256 devices in a mesh: tensor: 8 (over z), sibling: 16 (over y, x), replica: 2 (over core).
Axes of the slice: x: 4, y: 4, z: 8, core: 2. Of those that a mesh axis runs over, the one named last changes fastest.
Arguments:
- reply_x: bfloat16 [512, 8, 16384], P(('replica', 'sibling'), None, 'tensor'), parts along dimension 0, may hold values from -6 to 6
- reply_bc: bfloat16 [512, 8, 2, 2048], P(('replica', 'sibling'), None, None, 'tensor'), parts along dimension 0, may hold values from -6 to 6
- reply_dt: bfloat16 [512, 8, 256], P(('replica', 'sibling'), None, 'tensor'), parts along dimension 0, may hold values from -4 to 4
- reply_gate: bfloat16 [512, 8, 16384], P(('replica', 'sibling'), None, 'tensor'), parts along dimension 0, may hold values from -6 to 6
- reply_query: bfloat16 [512, 8, 8192], P(('replica', 'sibling'), None, 'tensor'), parts along dimension 0, may hold values from -40 to 40
- reply_kv: bfloat16 [512, 8, 2, 1024], P(('replica', 'sibling'), None, None, 'tensor'), parts along dimension 0, may hold values from -21 to 21
- lengths: int32 [512], P(('replica', 'sibling')), parts along dimension 0, may hold values from 1 to 8, 1280 in all
- fork_list: int32 [512, 1], P(('replica', 'sibling')), parts along dimension 0, may hold values from 0 to 15; in each aligned block of 16 rows (0 to 15, 16 to 31, ...) at most 2 rows name the same one
- ssm_state: float32 [32, 256, 64, 256], P(('replica', 'sibling'), 'tensor'), parts along dimension 0, may hold values from -1.2 to 1.2
- conv_x: bfloat16 [32, 3, 16384], P(('replica', 'sibling'), None, 'tensor'), parts along dimension 0, may hold values from -6 to 6
- conv_bc: bfloat16 [32, 3, 2, 2048], P(('replica', 'sibling'), None, None, 'tensor'), parts along dimension 0, may hold values from -6 to 6
- kv_pool: bfloat16 [1024, 128, 2, 1024], P(('replica', 'sibling'), None, None, 'tensor'), parts along dimension 0, may hold values from -16 to 16
- page_table: int32 [32, 16], P(('replica', 'sibling')), parts along dimension 0, may hold values from 0 to 31, as said below
- kernel_x: float32 [4, 16384], P(None, 'tensor'), may hold values from -2.5 to 2.5
- kernel_bc: float32 [4, 2, 2048], P(None, None, 'tensor'), may hold values from -2.5 to 2.5
- a_log: float32 [256], P('tensor'), may hold values from -1 to 1.5
- dt_bias: float32 [256], P('tensor'), may hold values from -4 to 0
- d_skip: float32 [256], P('tensor'), may hold values from 0.5 to 2
- norm_gain: float32 [16384], P('tensor'), may hold values from 0.1 to 1.9
Outputs:
- mamba_out: bfloat16 [512, 8, 16384], P(('replica', 'sibling'), None, 'tensor'), parts along dimension 0
- attn_out: bfloat16 [512, 8, 8192], P(('replica', 'sibling'), None, 'tensor'), parts along dimension 0
The draws below stay inside these ranges and needn't reach their ends.
There are 2 independent parts, one for each index of `replica`. The reference program is written for one: setup_inputs(seed, part) draws one part's arguments, and reference() takes and returns one part's arrays. A program takes and returns all parts, laid end to end along the dimension named above; an argument that names none is the same for every part. Nothing has to cross between parts.
Inputs may be any that keep to these rules, and one draw needn't show every extreme that they name: fork_list[c, 0] is the parent of child c. Among the 16 children of one device (aligned blocks of rows), no parent is named more than 2 times, and in every draw some parent is named exactly 2 times in some block; every parent has at least one child. `page_table`: the entries of each row are distinct; parent p's pool pages are rows p * 32 to p * 32 + 31 of kv_pool. `lengths`: the largest length is exactly 8.
All inputs are finite; a program needn't handle non-finite values. No bound on the sum of `lengths` on one device may be relied on, other than what follows from the above.
Results may differ from the reference program's by a relative error of at most 0.0048.
Values may be sent and summed in bfloat16 or wider, within the bound.
No kernel may reach another device: no remote copies, remote signals or barrier semaphores. Data moves between devices by JAX's collectives and lax.ppermute only.
A program may use at most 128 MiB of HBM per device.

```python
import math
import jax
import jax.numpy as jnp
import numpy as np
from jax import lax

MHEADS = 256
MHDIM = 64
NSTATE = 256
GROUPS = 8
CONVK = 4
QHEADS = 64
KVHEADS = 8
AHDIM = 128
CHILD_DEV = 16
CAP = 2
REPLY = 8
PREFIX = 2048
PAGE = 128
PAGES = 16
POOL = 32
PARENTS = 16
CHILDREN = 256


def draw_reply_query(key, part):
    key = jax.random.fold_in(key, 11)
    first_key = jax.random.fold_in(key, 0)
    values = jax.random.truncated_normal(first_key, -5.0, 5.0, (CHILDREN, REPLY, QHEADS, AHDIM), jnp.float32)
    return values.reshape(CHILDREN, REPLY, QHEADS * AHDIM).astype(jnp.bfloat16)


def draw_reply_kv(key, part):
    key = jax.random.fold_in(key, 37)
    first_key = jax.random.fold_in(key, 0)
    shape_all = (CHILDREN, REPLY, 2, KVHEADS, AHDIM)
    values = jax.random.truncated_normal(first_key, -5.0, 5.0, shape_all, jnp.float32)
    return values.reshape(CHILDREN, REPLY, 2, KVHEADS * AHDIM).astype(jnp.bfloat16)


def draw_kv_pool(key, part):
    key = jax.random.fold_in(key, 23)
    shape_all = (PARENTS * POOL, PAGE, 2, KVHEADS, AHDIM)
    values = jax.random.truncated_normal(key, -5.0, 5.0, shape_all, jnp.float32)
    return values.reshape(PARENTS * POOL, PAGE, 2, KVHEADS * AHDIM).astype(jnp.bfloat16)


def draw_page_table(key, part):
    key = jax.random.fold_in(key, 5)
    first_key, second_key = jax.random.split(key)
    order = jax.vmap(lambda one: jax.random.permutation(one, PAGES))(jax.random.split(first_key, PARENTS)).astype(jnp.int32)
    choose = jax.random.randint(second_key, (PARENTS, PAGES), 0, 2).astype(jnp.int32)
    row_ids = lax.broadcasted_iota(jnp.int32, (PARENTS, PAGES), 0)
    choose = jnp.where((row_ids == 0) & (order == PAGES - 1), 1, choose)
    choose = jnp.where((row_ids == 0) & (order == 0), 0, choose)
    return (2 * order + choose).astype(jnp.int32)


def steps_of(rng, extent, cuts, least, high):
    level = 1.0
    for dim, shards_of in cuts:
        draws = jax.random.uniform(jax.random.fold_in(jax.random.fold_in(rng, 6), dim), (shards_of,), jnp.float32, least / len(cuts), high / len(cuts))
        level = level * jnp.repeat(jnp.exp(draws), extent[dim] // shards_of).reshape((-1,) + (1,) * (len(extent) - 1 - dim))
    return level


def profile(amount, total, limit, lean):
    portions = [(1 << 20) // math.isqrt(grade ** lean) + 1 for grade in range(2, amount + 1)]
    rest, holding = total - limit - (amount - 1), [1] * (amount - 1)
    while rest > 0:
        free = [i for i in range(amount - 1) if holding[i] < limit]
        mass, remaining = sum([portions[i] for i in free]), rest
        for i in free:
            addition = min(limit - holding[i], max(1, remaining * portions[i] // mass), rest)
            holding[i] = holding[i] + addition
            rest = rest - addition
    return np.array([limit] + holding)


def uneven(stream_key, amount, total, bound, slope):
    if amount == 2:
        one = jax.random.randint(stream_key, (), max(1, total - bound), min(bound, total - 1) + 1)
        return jnp.stack([one, total - one])
    sizes = jnp.asarray(profile(amount, total, bound, slope), jnp.int32)
    couples = (amount - 1) // 2
    donor, taker = sizes[1:1 + 2 * couples:2], sizes[2:2 + 2 * couples:2]
    room = jnp.minimum(donor - 1, bound - taker)
    moved = jax.random.randint(jax.random.fold_in(stream_key, 1), (couples,), 0, 1 << 20) % (room + 1)
    sizes = sizes.at[1:1 + 2 * couples:2].set(donor - moved).at[2:2 + 2 * couples:2].set(taker + moved)
    return sizes[jax.random.permutation(jax.random.fold_in(stream_key, 2), amount)]


def deal_out(rng, own, number, rows, number_of, top, reach, skew):
    sequence = jax.random.permutation(rng, number_of)
    packed, common = portions_of(number_of, rows * top, reach, skew, True), portions_of(number_of, rows * top, reach, skew, False)
    places = jnp.arange(number_of)

    def named(tallies, turn):
        used = int((tallies > 0).sum())
        fixed = max(1, used // 4)
        passed = fixed + (places - fixed + turn * (used - fixed)) % max(1, number_of - fixed)
        return jnp.zeros((number_of,), jnp.int32).at[sequence[jnp.where(places < fixed, places, passed)]].set(jnp.asarray(tallies, jnp.int32))

    tallies = jnp.where(number % 4 == 0, named(packed, number // 4), named(common, number - number // 4 - 1))
    mixed = jax.random.permutation(jax.random.fold_in(own, 3), number_of)
    giver, receiver = mixed[0:number_of // 2 * 2:2], mixed[1:number_of // 2 * 2:2]
    margin = jnp.minimum(tallies[giver] - 1, reach - tallies[receiver]) // 2
    margin = jnp.where((giver == sequence[0]) | (receiver == sequence[0]) | (tallies[receiver] == 0), 0, jnp.maximum(margin, 0))
    passed = jax.random.randint(jax.random.fold_in(own, 4), (number_of // 2,), 0, 1 << 20) % (margin + 1)
    tallies = tallies.at[giver].add(-passed).at[receiver].add(passed)
    members = jnp.searchsorted(jnp.cumsum(tallies), jnp.arange(rows * top), side="right").astype(jnp.int32)
    table = members.reshape(top, rows).T
    table = table[jax.random.permutation(jax.random.fold_in(own, 1), rows)]
    turn = jax.random.randint(jax.random.fold_in(own, 2), (rows, 1), 0, top)
    return jnp.take_along_axis(table, (jnp.arange(top)[None, :] + turn) % top, axis=1)


def portions_of(count, total, reach, lean, full):
    loads = [(1 << 20) // math.isqrt(rank ** lean) + 1 for rank in range(1, count + 1)]
    largest = reach if full else min(reach, max(-(-total // count), total * loads[0] // sum(loads)))
    least = 1 if total - largest >= count - 1 else 0
    given, rest = [largest] + [least] * (count - 1), total - largest - least * (count - 1)
    while rest > 0:
        candidates = [i for i in range(1, count) if given[i] < largest] or [i for i in range(1, count) if given[i] < reach]
        pool, remaining = sum([loads[i] for i in candidates]), rest
        for i in candidates:
            more = min(reach - given[i], max(1, remaining * loads[i] // pool), rest)
            given[i] = given[i] + more
            rest = rest - more
    return np.array(given)


def bell_draw(rng, shape, scale, most, shards=(), kind=jnp.bfloat16):
    array = scale * jax.random.normal(rng, shape, jnp.float32)
    if shards:
        array = array * steps_of(rng, shape, shards, -0.22, 0.18)
    return jnp.clip(array, -most, most).astype(kind)


def setup_inputs(seed: int = 0, part: int = 0) -> dict:
    key_of = jax.random.split(jax.random.key(seed), 20)
    part_splits = jax.random.split(jax.random.fold_in(key_of[19], part), 20)
    reply_x = bell_draw(part_splits[0], (CHILDREN, REPLY, MHEADS * MHDIM), 1.0, 6.0, ((0, 16), (2, 8)))
    reply_bc = bell_draw(part_splits[1], (CHILDREN, REPLY, 2, GROUPS * NSTATE), 1.0, 6.0, ((0, 16), (3, 8)))
    reply_dt = bell_draw(part_splits[2], (CHILDREN, REPLY, MHEADS), 1.0, 4.0, ((0, 16), (2, 8)))
    reply_gate = bell_draw(part_splits[3], (CHILDREN, REPLY, MHEADS * MHDIM), 1.0, 6.0, ((0, 16), (2, 8)))
    reply_query = draw_reply_query(jax.random.fold_in(jax.random.fold_in(key_of[19], part), 71), part)
    reply_kv = draw_reply_kv(jax.random.fold_in(jax.random.fold_in(key_of[19], part), 71), part)
    lengths = uneven(part_splits[6], CHILDREN, CHILDREN * REPLY * 5 // 8, REPLY, 2).astype(jnp.int32)
    fork_list_keys = jax.random.split(jax.random.fold_in(part_splits[7], 1), CHILDREN // CHILD_DEV)
    fork_list_turns = jax.random.permutation(jax.random.fold_in(part_splits[7], 3), CHILDREN // CHILD_DEV)
    fork_list = jax.vmap(lambda own, number: deal_out(jax.random.fold_in(part_splits[7], 2), own, number, CHILD_DEV, PARENTS, 1, CAP, 1))(fork_list_keys, fork_list_turns).reshape((CHILDREN, 1))
    ssm_state = bell_draw(part_splits[8], (PARENTS, MHEADS, MHDIM, NSTATE), 0.2, 1.2, ((0, 16), (1, 8)), jnp.float32)
    conv_x = bell_draw(part_splits[9], (PARENTS, CONVK - 1, MHEADS * MHDIM), 1.0, 6.0, ((0, 16), (2, 8)))
    conv_bc = bell_draw(part_splits[10], (PARENTS, CONVK - 1, 2, GROUPS * NSTATE), 1.0, 6.0, ((0, 16), (3, 8)))
    kv_pool = draw_kv_pool(jax.random.fold_in(jax.random.fold_in(key_of[19], part), 71), part)
    page_table = draw_page_table(jax.random.fold_in(jax.random.fold_in(key_of[19], part), 71), part)
    kernel_x = bell_draw(key_of[13], (CONVK, MHEADS * MHDIM), 0.5, 2.5, ((1, 8),), jnp.float32)
    kernel_bc = bell_draw(key_of[14], (CONVK, 2, GROUPS * NSTATE), 0.5, 2.5, ((2, 8),), jnp.float32)
    a_log = jnp.clip(-1.0 + 2.5 * jax.random.uniform(key_of[15], (MHEADS,), jnp.float32) ** steps_of(key_of[15], (MHEADS,), ((0, 8),), -0.2, 0.2), -1.0, 1.5)
    dt_bias = jnp.clip(-4.0 + 4.0 * jax.random.uniform(key_of[16], (MHEADS,), jnp.float32) ** steps_of(key_of[16], (MHEADS,), ((0, 8),), -0.2, 0.2), -4.0, 0.0)
    d_skip = jnp.clip(0.5 + 1.5 * jax.random.uniform(key_of[17], (MHEADS,), jnp.float32) ** steps_of(key_of[17], (MHEADS,), ((0, 8),), -0.2, 0.2), 0.5, 2.0)
    norm_gain = jnp.clip(1.0 + 0.18 * jax.random.normal(key_of[18], (MHEADS * MHDIM,), jnp.float32), 0.1, 1.9)
    return {"reply_x": reply_x, "reply_bc": reply_bc, "reply_dt": reply_dt, "reply_gate": reply_gate, "reply_query": reply_query, "reply_kv": reply_kv, "lengths": lengths, "fork_list": fork_list, "ssm_state": ssm_state, "conv_x": conv_x, "conv_bc": conv_bc, "kv_pool": kv_pool, "page_table": page_table, "kernel_x": kernel_x, "kernel_bc": kernel_bc, "a_log": a_log, "dt_bias": dt_bias, "d_skip": d_skip, "norm_gain": norm_gain}


HIGH = lax.Precision.HIGHEST
NEGATIVE = -1e+30
EPSILON = 1e-05

def causal_conv(history, incoming, kernel):
    joined = jnp.concatenate([history, incoming], axis=0).astype(jnp.float32)
    span_len = incoming.shape[0]
    summed = joined[0:span_len] * kernel[0]
    for offset in range(1, kernel.shape[0]):
        summed = summed + joined[offset:offset + span_len] * kernel[offset]
    return jax.nn.silu(summed)

def state_space(xconv, bmat, cmat, dt_raw, start, a_log, dt_bias, d_skip, head_share):
    span_len = xconv.shape[0]
    groups_here = bmat.shape[1]
    heads_here = dt_raw.shape[1]
    head_size = xconv.shape[1] // heads_here
    xsplit = xconv.reshape(span_len, groups_here, head_share, head_size)
    step_size = jax.nn.softplus(dt_raw.astype(jnp.float32) + dt_bias)
    decays = (step_size * -jnp.exp(a_log)).reshape(span_len, groups_here, head_share)
    running = jnp.cumsum(decays, axis=0)
    anchor = start.reshape(groups_here, head_share, head_size, -1)
    carried = jnp.einsum('tgn,gpdn->tgpd', cmat, anchor, precision=HIGH) * jnp.exp(running)[:, :, :, None]
    intersection = jnp.einsum('tgn,sgn->gts', cmat, bmat, precision=HIGH)
    causal = lax.broadcasted_iota(jnp.int32, (span_len, span_len), 0) >= lax.broadcasted_iota(jnp.int32, (span_len, span_len), 1)
    running_t = jnp.transpose(running, (1, 2, 0))
    spread = running_t[:, :, :, None] - running_t[:, :, None, :]
    kernel_ts = jnp.where(causal, jnp.exp(jnp.where(causal, spread, 0.0)), 0.0)
    steps_dt = jnp.transpose(step_size.reshape(span_len, groups_here, head_share), (1, 2, 0))
    weight = kernel_ts * steps_dt[:, :, None, :] * intersection[:, None]
    within = jnp.einsum('gpts,sgpd->tgpd', weight, xsplit, precision=HIGH)
    direct = d_skip.reshape(groups_here, head_share)[None, :, :, None] * xsplit
    return (carried + within + direct).reshape(span_len, heads_here * head_size)

def full_attention(queries, prefix_keys, prefix_values, new_keys, new_values):
    span_len = queries.shape[0]
    kv_heads = prefix_keys.shape[-1] // AHDIM
    grouped = queries.reshape(span_len, kv_heads, -1, AHDIM).astype(jnp.float32)
    inverse_root = AHDIM ** (-0.5)
    keys_old = prefix_keys.reshape(-1, kv_heads, AHDIM).astype(jnp.float32)
    values_old = prefix_values.reshape(-1, kv_heads, AHDIM).astype(jnp.float32)
    keys_new = new_keys.reshape(-1, kv_heads, AHDIM).astype(jnp.float32)
    values_new = new_values.reshape(-1, kv_heads, AHDIM).astype(jnp.float32)
    prefix_scores = jnp.einsum('tgqd,lgd->gqtl', grouped, keys_old, precision=HIGH) * inverse_root
    reply_scores = jnp.einsum('tgqd,lgd->gqtl', grouped, keys_new, precision=HIGH) * inverse_root
    causal = lax.broadcasted_iota(jnp.int32, (span_len, span_len), 0) >= lax.broadcasted_iota(jnp.int32, (span_len, span_len), 1)
    reply_scores = jnp.where(causal, reply_scores, NEGATIVE)
    highest = jnp.maximum(lax.optimization_barrier(jnp.max(prefix_scores, axis=-1)), lax.optimization_barrier(jnp.max(reply_scores, axis=-1)))
    prefix_raw = jnp.exp(prefix_scores - highest[..., None])
    reply_raw = jnp.exp(reply_scores - highest[..., None])
    denominator = lax.optimization_barrier(jnp.sum(prefix_raw, axis=-1)) + lax.optimization_barrier(jnp.sum(reply_raw, axis=-1))
    prefix_weights = lax.optimization_barrier(prefix_raw.astype(jnp.bfloat16)).astype(jnp.float32)
    reply_weights = lax.optimization_barrier(reply_raw.astype(jnp.bfloat16)).astype(jnp.float32)
    summed = jnp.einsum('gqtl,lgd->tgqd', prefix_weights, values_old, precision=HIGH)
    summed = summed + jnp.einsum('gqtl,lgd->tgqd', reply_weights, values_new, precision=HIGH)
    return (summed / jnp.transpose(denominator, (2, 0, 1))[..., None]).reshape(span_len, -1)

def reference(reply_x, reply_bc, reply_dt, reply_gate, reply_query, reply_kv, lengths, fork_list, ssm_state, conv_x, conv_bc, kv_pool, page_table, kernel_x, kernel_bc, a_log, dt_bias, d_skip, norm_gain):
    head_share = MHEADS // GROUPS

    def one_child(items):
        inputs_x, inputs_bc, inputs_dt, gates, queries, news, length, parent = items
        xconv = causal_conv(conv_x[parent], inputs_x, kernel_x)
        bcconv = causal_conv(conv_bc[parent], inputs_bc, kernel_bc)
        bmat = bcconv[:, 0].reshape(REPLY, GROUPS, NSTATE)
        cmat = bcconv[:, 1].reshape(REPLY, GROUPS, NSTATE)
        mixed = state_space(xconv, bmat, cmat, inputs_dt, ssm_state[parent], a_log, dt_bias, d_skip, head_share)
        mixer = lax.optimization_barrier(mixed.astype(jnp.bfloat16)).astype(jnp.float32)
        gated = mixer * jax.nn.silu(gates.astype(jnp.float32))
        grouped = gated.reshape(REPLY, GROUPS, -1)
        meansq = lax.optimization_barrier(jnp.mean(grouped * grouped, axis=-1, keepdims=True))
        normed = (grouped * lax.rsqrt(meansq + EPSILON) * norm_gain.reshape(GROUPS, -1)).reshape(REPLY, -1)
        page_rows = (parent * POOL + page_table[parent]).astype(jnp.int32)
        pages = kv_pool[page_rows].reshape(PREFIX, 2, -1)
        attended = full_attention(queries, pages[:, 0], pages[:, 1], news[:, 0], news[:, 1])
        valid = jnp.arange(REPLY, dtype=jnp.int32) < length
        mamba_rows = jnp.where(valid[:, None], normed, 0.0).astype(jnp.bfloat16)
        attn_rows = jnp.where(valid[:, None], attended, 0.0).astype(jnp.bfloat16)
        return (mamba_rows, attn_rows)
    mamba_out, attn_out = lax.map(one_child, (reply_x, reply_bc, reply_dt, reply_gate, reply_query, reply_kv, lengths, fork_list[:, 0]))
    return (mamba_out, attn_out)
```

```python
import math

import jax
import jax.numpy as jnp
from jax import lax
from jax.experimental import pallas as pl
from jax.experimental.pallas import tpu as pltpu
from jax.sharding import PartitionSpec as P

AHDIM = 128
CAP = 2
NEGATIVE = -1e30
EPSILON = 1e-05
F32 = jnp.float32
BF16 = jnp.bfloat16

Q_ROWS = 64
KV_ROWS = 16
C_ROWS = 16
SLOT_ROWS = Q_ROWS + KV_ROWS + C_ROWS
HIST_AT = CAP * SLOT_ROWS
HIST_ROWS = 80
SEND_ROWS = HIST_AT + HIST_ROWS
LIMIT = 50 * 1024 * 1024


def whole(memory_space=pltpu.VMEM):
    return pl.BlockSpec(memory_space=memory_space)


def silu(v):
    return v / (1.0 + jnp.exp(-v))


def fold(x, rows):
    return jnp.concatenate([x[:, i : i + 128] for i in range(0, x.shape[1], 128)], axis=0)


def unfold(x, rows):
    return jnp.concatenate([x[i : i + rows] for i in range(0, x.shape[0], rows)], axis=1)


def place_of(fork, count, child):
    parent = fork[child, 0]
    rank = jnp.minimum(count[parent], CAP - 1)
    count[parent] = count[parent] + 1
    return parent, rank


def clear(count):
    for parent in range(count.shape[0]):
        count[parent] = 0


def spread_bc(bc, rows_bc):
    for i, part in enumerate(rows_bc):
        part[...] = bc[:, :, 128 * i : 128 * i + 128].astype(F32).reshape(part.shape)


def pack_kernel(fork, query, news, bc, conv_x, conv_bc, send, count, *rows_bc):
    children = query.shape[0]
    clear(count)
    send[:, 0:HIST_AT, :] = jnp.zeros((send.shape[0], HIST_AT, 128), BF16)
    spread_bc(bc, rows_bc)
    own_x = conv_x[0].astype(F32)
    pairs = [conv_bc[0, row].astype(F32) for row in range(3)]
    own_b = jnp.concatenate([pair[0:1] for pair in pairs], axis=0)
    own_c = jnp.concatenate([pair[1:2] for pair in pairs], axis=0)
    own = jnp.concatenate([own_x, own_b, own_c], axis=1)
    own = jnp.concatenate([own, jnp.zeros((1, own.shape[1]), F32)], axis=0)
    history = fold(own, 4).astype(BF16)
    for parent in range(send.shape[0]):
        send[parent, HIST_AT:SEND_ROWS, :] = history
    for child in range(children):
        parent, rank = place_of(fork, count, child)
        rows_q = fold(query[child].astype(F32), 8).astype(BF16)
        rows_c = [part[pl.ds(16 * child + 1, 8, stride=2), :] for part in rows_bc]
        rows_c = jnp.concatenate(rows_c, axis=0).astype(BF16)
        block = jnp.concatenate([rows_q, news[child], rows_c], axis=0)
        send[parent, pl.ds(pl.multiple_of(rank * SLOT_ROWS, 32), SLOT_ROWS), :] = block


def prefix_kernel(table, page, state, keys, values, state_hi, state_lo, rows):
    rows[...] = page[0].astype(F32)
    keys[...] = rows[pl.ds(0, 128, stride=2), :].astype(BF16)
    values[:, 0:128] = rows[pl.ds(1, 128, stride=2), :].astype(BF16)
    values[:, 128:256] = jnp.ones((128, 128), BF16)
    high = state[...].astype(BF16)
    state_hi[...] = high
    state_lo[...] = (state[...] - high.astype(F32)).astype(BF16)


def transposed_dot(a, b):
    return lax.dot_general(a, b, (((1,), (1,)), ((), ())), preferred_element_type=F32)


def parent_kernel(got, keys, values, state_hi, state_lo, conv_bc, kernel_bc, back, rows):
    senders = got.shape[0]
    raw = []
    for slot in range(CAP):
        at = slot * SLOT_ROWS + Q_ROWS + KV_ROWS
        part = got[:, at : at + C_ROWS, :].astype(F32)
        raw.append(jnp.concatenate([part[:, 0:8], part[:, 8:16]], axis=2))
    raw = jnp.concatenate(raw, axis=1).reshape(senders * CAP * 8, 256)
    old = [conv_bc[0, row].astype(F32)[1:2] for row in range(3)]
    token = lax.broadcasted_iota(jnp.int32, (senders * CAP, 8, 256), 1)
    taps = [kernel_bc[tap][1:2] for tap in range(4)]
    total = raw * taps[3]
    for lag in range(1, 4):
        early = jnp.concatenate(old[3 - lag :] + [jnp.zeros((8 - lag, 256), F32)], axis=0)
        moved = pltpu.roll(raw, lag, 0).reshape(senders * CAP, 8, 256)
        joined = jnp.where(token < lag, early[None], moved).reshape(raw.shape)
        total = total + joined * taps[3 - lag]
    cmat = silu(total)
    c_hi = cmat.astype(BF16)
    c_lo = (cmat - c_hi.astype(F32)).astype(BF16)
    channels = state_hi.shape[0]
    for at in range(0, channels, 256):
        high = state_hi[at : at + 256, :]
        read = transposed_dot(c_hi, high) + transposed_dot(c_lo, high)
        read = read + transposed_dot(c_hi, state_lo[at : at + 256, :])
        back[:, :, :, at : at + 256] = read.astype(BF16).reshape(senders, CAP, 8, 256)

    factor = AHDIM**-0.5 * math.log2(math.e)
    row_ids = lax.broadcasted_iota(jnp.int32, (256, 32), 0)
    col_ids = lax.broadcasted_iota(jnp.int32, (256, 32), 1)
    seen = jnp.logical_and(row_ids // 64 == col_ids // 8, row_ids % 8 >= col_ids % 8)

    def block(step, carry):
        sender = 2 * step
        places = [(sender + i, slot * SLOT_ROWS) for i in range(2) for slot in range(CAP)]
        queries = jnp.concatenate([got[s, at : at + Q_ROWS, :] for s, at in places], axis=0)
        at_kv = [(s, at + Q_ROWS) for s, at in places]
        rows[...] = jnp.concatenate(
            [got[s, at : at + KV_ROWS, :].astype(F32) for s, at in at_kv], axis=0
        )
        new_keys = rows[pl.ds(0, 32, stride=2), :].astype(BF16)
        new_values = rows[pl.ds(1, 32, stride=2), :].astype(BF16)
        new_values = jnp.concatenate([new_values, jnp.ones((32, 128), BF16)], axis=1)
        scores = transposed_dot(queries, keys[...])
        reply = jnp.where(seen, transposed_dot(queries, new_keys), NEGATIVE)
        highest = jnp.maximum(
            jnp.max(scores, axis=1, keepdims=True), jnp.max(reply, axis=1, keepdims=True)
        )
        weights = jnp.exp2((scores - highest) * factor).astype(BF16)
        reply_weights = jnp.exp2((reply - highest) * factor).astype(BF16)
        summed = jnp.dot(weights, values[...], preferred_element_type=F32)
        summed = summed + jnp.dot(reply_weights, new_values, preferred_element_type=F32)
        attended = summed[:, 0:128] / summed[:, 128:256]
        for i in range(2 * CAP):
            one = unfold(attended[64 * i : 64 * i + 64], 8)
            back[sender + i // CAP, i % CAP, :, channels:] = one.astype(BF16)
        return carry

    lax.fori_loop(0, senders // 2, block, 0)


def child_kernel(
    fork, got, reply_x, bc, dt, gate, kernel_x, kernel_bc, params,
    within, fade, gates, history, weights, *rows_bc,
):
    children = reply_x.shape[0]
    count = children * 8
    for child in range(children):
        own = got[fork[child, 0], HIST_AT:SEND_ROWS, :].astype(F32)
        history[8 * child : 8 * child + 4, :] = unfold(own, 4)
        history[8 * child + 4 : 8 * child + 8, :] = jnp.zeros((4, history.shape[1]), F32)

    def convolve(raw, old, taps):
        token = lax.broadcasted_iota(jnp.int32, raw.shape, 0) % 8
        total = raw * taps[3]
        for lag in range(1, 4):
            early = old if lag == 3 else pltpu.roll(old, count - (3 - lag), 0)
            joined = jnp.where(token < lag, early, pltpu.roll(raw, lag, 0))
            total = total + joined * taps[3 - lag]
        return silu(total)

    spread_bc(bc, rows_bc)
    channels = reply_x.shape[2]
    state = bc.shape[2]
    mats = []
    for part in range(2):
        raw = [half[pl.ds(part, count, stride=2), :] for half in rows_bc]
        raw = jnp.concatenate(raw, axis=1)
        at = channels + part * state
        taps = [kernel_bc[tap][part : part + 1] for tap in range(4)]
        mats.append(convolve(raw, history[:, at : at + state], taps))
    bmat = mats[0].reshape(children, 8, state)
    cmat = mats[1].reshape(children, 8, state)

    heads = dt.shape[2]
    spread = lax.broadcasted_iota(jnp.int32, (heads, 128), 1) % heads
    spread = (spread == lax.broadcasted_iota(jnp.int32, (heads, 128), 0)).astype(BF16)
    raw_dt = jnp.dot(
        dt[...].astype(F32).reshape(count, heads).astype(BF16), spread, preferred_element_type=F32
    )
    shifted = raw_dt + params[1:2]
    step_size = jnp.maximum(shifted, 0.0) + jnp.log1p(jnp.exp(-jnp.abs(shifted)))
    running = step_size * -jnp.exp(params[0:1])
    token = lax.broadcasted_iota(jnp.int32, (count, 128), 0) % 8
    for hop in (1, 2, 4):
        running = running + jnp.where(token >= hop, pltpu.roll(running, hop, 0), 0.0)
    lane = lax.broadcasted_iota(jnp.int32, (count, 128), 1) // heads

    def put(at, value):
        high = value.astype(BF16).astype(F32)
        rest = value - high
        middle = rest.astype(BF16).astype(F32)
        low = rest - middle
        parts = jnp.where(lane == 0, high, jnp.where(lane == 1, middle, jnp.where(lane == 2, low, 0.0)))
        weights[at * count : (at + 1) * count, :] = parts.astype(BF16)

    token3 = lax.broadcasted_iota(jnp.int32, (children, 8, 128), 1)
    running3 = running.reshape(children, 8, 128)
    step3 = step_size.reshape(children, 8, 128)
    skip = params[2:3][None]
    for source in range(8):
        overlap = jnp.sum(cmat * bmat[:, source : source + 1, :], axis=2, keepdims=True)
        later = token3 >= source
        span = jnp.where(later, running3 - running3[:, source : source + 1, :], 0.0)
        value = jnp.where(later, jnp.exp(span) * step3[:, source : source + 1, :] * overlap, 0.0)
        value = value + jnp.where(token3 == source, skip, 0.0)
        put(source, value.reshape(count, 128))
    put(8, jnp.exp(running))

    per = 256
    for at in range(0, channels, per):
        raw = reply_x[:, :, at : at + per].astype(F32).reshape(count, per)
        taps = [kernel_x[tap : tap + 1, at : at + per] for tap in range(4)]
        xconv = convolve(raw, history[:, at : at + per], taps).reshape(children, 8, per)
        head = at // 64 + lax.broadcasted_iota(jnp.int32, (128, per), 1) // 64
        source_head = lax.broadcasted_iota(jnp.int32, (128, per), 0) % heads
        spread_x = (head == source_head).astype(BF16)
        wide = jnp.dot(weights[...], spread_x, preferred_element_type=F32)
        total = None
        for source in range(8):
            weight = wide[source * count : (source + 1) * count].reshape(children, 8, per)
            term = weight * xconv[:, source : source + 1, :]
            total = term if total is None else total + term
        within[:, :, at : at + per] = total
        fade[:, :, at : at + per] = wide[8 * count :].reshape(children, 8, per)
        gates[:, :, at : at + per] = silu(gate[:, :, at : at + per].astype(F32))


def finish_kernel(fork, lengths, got, within, fade, gates, gain, mamba, attn, count):
    clear(count)
    channels = within.shape[2]
    for child in range(within.shape[0]):
        parent, rank = place_of(fork, count, child)
        length = lengths[child]
        read = got[parent, rank].astype(F32)
        mixer = fade[child] * read[:, 0:channels] + within[child]
        gated = mixer.astype(BF16).astype(F32) * gates[child]
        meansq = jnp.mean(gated * gated, axis=1, keepdims=True)
        normed = gated * lax.rsqrt(meansq + EPSILON) * gain[...]
        token = lax.broadcasted_iota(jnp.int32, (8, 1), 0)
        mamba[child] = jnp.where(token < length, normed, 0.0).astype(BF16)
        attn[child] = jnp.where(token < length, read[:, channels:], 0.0).astype(BF16)


def params_of(flops, bytes_accessed, transcendentals=0):
    return dict(
        compiler_params=pltpu.CompilerParams(vmem_limit_bytes=LIMIT),
        cost_estimate=pl.CostEstimate(
            flops=flops, bytes_accessed=bytes_accessed, transcendentals=transcendentals
        ),
    )


def local(
    reply_x,
    reply_bc,
    reply_dt,
    reply_gate,
    reply_query,
    reply_kv,
    lengths,
    fork_list,
    ssm_state,
    conv_x,
    conv_bc,
    kv_pool,
    page_table,
    kernel_x,
    kernel_bc,
    a_log,
    dt_bias,
    d_skip,
    norm_gain,
):
    children, tokens, channels = reply_x.shape
    siblings = lax.axis_size("sibling")
    state = ssm_state.shape[3]
    widths = reply_query.shape[2]
    heads = a_log.shape[0]
    news = reply_kv.reshape(children, 2 * tokens, AHDIM)
    bc = reply_bc.reshape(children, 2 * tokens, state)
    pool = kv_pool.reshape(kv_pool.shape[0], 256, AHDIM)
    flat_state = ssm_state.reshape(channels, state)
    params = jnp.tile(jnp.stack([a_log, dt_bias, d_skip]), (1, 128 // heads))
    gain = norm_gain.reshape(1, channels)

    halves = [pltpu.VMEM((children * 2 * tokens, 128), F32)] * (state // 128)

    send = pl.pallas_call(
        pack_kernel,
        out_shape=jax.ShapeDtypeStruct((siblings, SEND_ROWS, 128), BF16),
        in_specs=[whole(pltpu.SMEM)] + [whole()] * 5,
        out_specs=whole(),
        scratch_shapes=[pltpu.SMEM((siblings,), jnp.int32)] + halves,
        **params_of(1_000_000, 2_000_000),
    )(fork_list, reply_query, news, bc, conv_x, conv_bc)
    got = lax.all_to_all(send, "sibling", split_axis=0, concat_axis=0, tiled=True)

    pages = page_table.shape[1]
    share = channels // pages
    keys, values, state_hi, state_lo = pl.pallas_call(
        prefix_kernel,
        out_shape=(
            jax.ShapeDtypeStruct((pages * 128, AHDIM), BF16),
            jax.ShapeDtypeStruct((pages * 128, 2 * AHDIM), BF16),
            jax.ShapeDtypeStruct((channels, state), BF16),
            jax.ShapeDtypeStruct((channels, state), BF16),
        ),
        grid_spec=pltpu.PrefetchScalarGridSpec(
            num_scalar_prefetch=1,
            grid=(pages,),
            in_specs=[
                pl.BlockSpec((1, 256, AHDIM), lambda i, table: (table[0, i], 0, 0)),
                pl.BlockSpec((share, state), lambda i, table: (i, 0)),
            ],
            out_specs=[
                pl.BlockSpec((128, AHDIM), lambda i, table: (i, 0)),
                pl.BlockSpec((128, 2 * AHDIM), lambda i, table: (i, 0)),
                pl.BlockSpec((share, state), lambda i, table: (i, 0)),
                pl.BlockSpec((share, state), lambda i, table: (i, 0)),
            ],
            scratch_shapes=[pltpu.VMEM((256, AHDIM), F32)],
        ),
        **params_of(4_000_000, 8_000_000),
    )(page_table, pool, flat_state)

    back = pl.pallas_call(
        parent_kernel,
        out_shape=jax.ShapeDtypeStruct((siblings, CAP, tokens, channels + widths), BF16),
        in_specs=[whole()] * 7,
        out_specs=whole(),
        scratch_shapes=[pltpu.VMEM((64, AHDIM), F32)],
        **params_of(6_000_000_000, 8_000_000, 4_000_000),
    )(got, keys, values, state_hi, state_lo, conv_bc, kernel_bc)
    returned = lax.all_to_all(back, "sibling", split_axis=0, concat_axis=0, tiled=True)

    wide = jax.ShapeDtypeStruct((children, tokens, channels), F32)
    within, fade, gates = pl.pallas_call(
        child_kernel,
        out_shape=(wide, wide, wide),
        in_specs=[whole(pltpu.SMEM)] + [whole()] * 8,
        out_specs=(whole(), whole(), whole()),
        scratch_shapes=[
            pltpu.VMEM((children * tokens, channels + 2 * state), F32),
            pltpu.VMEM((9 * children * tokens, 128), BF16),
        ]
        + halves,
        **params_of(600_000_000, 8_000_000, 1_000_000),
    )(fork_list, got, reply_x, bc, reply_dt, reply_gate, kernel_x, kernel_bc, params)

    return pl.pallas_call(
        finish_kernel,
        out_shape=(
            jax.ShapeDtypeStruct((children, tokens, channels), BF16),
            jax.ShapeDtypeStruct((children, tokens, widths), BF16),
        ),
        in_specs=[whole(pltpu.SMEM), whole(pltpu.SMEM)] + [whole()] * 5,
        out_specs=(whole(), whole()),
        scratch_shapes=[pltpu.SMEM((siblings,), jnp.int32)],
        **params_of(10_000_000, 6_000_000),
    )(fork_list, lengths, returned, within, fade, gates, gain)


def solution(mesh):
    return jax.shard_map(
        local,
        mesh=mesh,
        in_specs=(
            P(("replica", "sibling"), None, "tensor"),
            P(("replica", "sibling"), None, None, "tensor"),
            P(("replica", "sibling"), None, "tensor"),
            P(("replica", "sibling"), None, "tensor"),
            P(("replica", "sibling"), None, "tensor"),
            P(("replica", "sibling"), None, None, "tensor"),
            P(("replica", "sibling")),
            P(("replica", "sibling"), None),
            P(("replica", "sibling"), "tensor", None, None),
            P(("replica", "sibling"), None, "tensor"),
            P(("replica", "sibling"), None, None, "tensor"),
            P(("replica", "sibling"), None, None, "tensor"),
            P(("replica", "sibling"), None),
            P(None, "tensor"),
            P(None, None, "tensor"),
            P("tensor"),
            P("tensor"),
            P("tensor"),
            P("tensor"),
        ),
        out_specs=(
            P(("replica", "sibling"), None, "tensor"),
            P(("replica", "sibling"), None, "tensor"),
        ),
        check_vma=False,
    )
```

```python
import math

import jax
import jax.numpy as jnp
from jax import lax
from jax.experimental import pallas as pl
from jax.experimental.pallas import tpu as pltpu
from jax.sharding import PartitionSpec as P

AHDIM = 128
CAP = 2
PREFIX_ARRAYS = 32
HISTORY_ROOM = 1024
NEGATIVE = -1e30
EPSILON = 1e-05
F32 = jnp.float32
BF16 = jnp.bfloat16

Q_ROWS = 64
KV_ROWS = 16
C_ROWS = 16
SLOT_ROWS = Q_ROWS + KV_ROWS + C_ROWS
HIST_AT = CAP * SLOT_ROWS
HIST_ROWS = 64
SEND_ROWS = HIST_AT + HIST_ROWS


def whole(memory_space=pltpu.VMEM):
    return pl.BlockSpec(memory_space=memory_space)


def silu(v):
    return v / (1.0 + jnp.exp(-v))


def fold(x, rows):
    return jnp.concatenate([x[:, i : i + 128] for i in range(0, x.shape[1], 128)], axis=0)


def unfold(x, rows):
    return jnp.concatenate([x[i : i + rows] for i in range(0, x.shape[0], rows)], axis=1)


def place_of(fork, count, child):
    parent = fork[child]
    rank = jnp.minimum(count[parent], CAP - 1)
    count[parent] = count[parent] + 1
    return parent, rank


def clear(count):
    for parent in range(count.shape[0]):
        count[parent] = 0


def bc_rows(rows_bc, part, at, count):
    start = 4 * at + part
    return [rows_bc[pl.ds(start + 2 * half, count, stride=4), :] for half in range(2)]


def pack_kernel(*refs):
    sources, (send, count), held, (sems, rows_bc) = refs[:6], refs[6:8], refs[8:14], refs[14:]
    copies = [
        pltpu.make_async_copy(source, kept, sems.at[i])
        for i, (source, kept) in enumerate(zip(sources, held))
    ]
    for copy in copies:
        copy.start()
    bc, conv_x, conv_bc, fork, query, news = held
    children = query.shape[0]
    clear(count)
    send[:, 0:HIST_AT, :] = jnp.zeros((send.shape[0], HIST_AT, 128), BF16)
    for copy in copies[:3]:
        copy.wait()
    rows_bc[...] = bc[...].astype(F32).reshape(rows_bc.shape)
    own_x = conv_x[0].astype(F32)
    pairs = [conv_bc[0, row].astype(F32) for row in range(3)]
    own_b = jnp.concatenate([pair[0:1] for pair in pairs], axis=0)
    own_c = jnp.concatenate([pair[1:2] for pair in pairs], axis=0)
    own = jnp.concatenate([own_x, own_b, own_c], axis=1)
    history = jnp.concatenate([fold(own, 3), jnp.zeros((4, 128), F32)], axis=0).astype(BF16)
    for parent in range(send.shape[0]):
        send[parent, HIST_AT:SEND_ROWS, :] = history
    for copy in copies[3:]:
        copy.wait()
    for child in range(children):
        parent, rank = place_of(fork, count, child)
        rows_q = fold(query[child].astype(F32), 8).astype(BF16)
        rows_c = jnp.concatenate(bc_rows(rows_bc, 1, 8 * child, 8), axis=0).astype(BF16)
        block = jnp.concatenate([rows_q, news[child], rows_c], axis=0)
        send[parent, pl.ds(pl.multiple_of(rank * SLOT_ROWS, 32), SLOT_ROWS), :] = block


def prefix_kernel(table, page, prefix, rows):
    rows[...] = page[0].astype(F32)
    for part in range(2):
        prefix[part] = rows[pl.ds(part, 128, stride=2), :].astype(BF16)


def transposed_dot(a, b):
    return lax.dot_general(a, b, (((1,), (1,)), ((), ())), preferred_element_type=F32)


def parent_kernel(
    got, conv_bc, kernel_bc, prefix_hbm, state_hbm, back, history,
    keys, values, state, read_rows, attn_rows, rows, sems, sems_out,
):
    senders = got.shape[0]
    pairs = [
        (prefix_hbm.at[0], keys),
        (prefix_hbm.at[1], values.at[:, pl.ds(0, 128)]),
        (state_hbm, state),
    ]
    loads = [pltpu.make_async_copy(*pair, sems.at[i]) for i, pair in enumerate(pairs)]
    for load in loads:
        load.start()
    old_rows = got.at[:, pl.ds(HIST_AT, HIST_ROWS), :]
    outs = [pltpu.make_async_copy(old_rows, history.at[pl.ds(0, senders)], sems_out.at[0])]
    outs[0].start()
    values[:, 128:256] = jnp.ones((values.shape[0], 128), BF16)
    raw = []
    for slot in range(CAP):
        at = slot * SLOT_ROWS + Q_ROWS + KV_ROWS
        part = got[:, at : at + C_ROWS, :].astype(F32)
        raw.append(jnp.concatenate([part[:, 0:8], part[:, 8:16]], axis=2))
    raw = jnp.concatenate(raw, axis=1).reshape(senders * CAP * 8, 256)
    old = [conv_bc[0, row].astype(F32)[1:2] for row in range(3)]
    token = lax.broadcasted_iota(jnp.int32, (senders * CAP, 8, 256), 1)
    taps = [kernel_bc[tap][1:2] for tap in range(4)]
    total = raw * taps[3]
    for lag in range(1, 4):
        early = jnp.concatenate(old[3 - lag :] + [jnp.zeros((8 - lag, 256), F32)], axis=0)
        moved = pltpu.roll(raw, lag, 0).reshape(senders * CAP, 8, 256)
        joined = jnp.where(token < lag, early[None], moved).reshape(raw.shape)
        total = total + joined * taps[3 - lag]
    cmat = silu(total)
    c_hi = cmat.astype(BF16)
    c_lo = (cmat - c_hi.astype(F32)).astype(BF16)
    channels = state.shape[0]

    factor = AHDIM**-0.5 * math.log2(math.e)
    row_ids = lax.broadcasted_iota(jnp.int32, (256, 32), 0)
    col_ids = lax.broadcasted_iota(jnp.int32, (256, 32), 1)
    seen = jnp.logical_and(row_ids // 64 == col_ids // 8, row_ids % 8 >= col_ids % 8)
    for load in loads[0:2]:
        load.wait()

    def attend(at):
        sender = 2 * at
        places = [(sender + i, slot * SLOT_ROWS) for i in range(2) for slot in range(CAP)]
        queries = jnp.concatenate([got[s, at : at + Q_ROWS, :] for s, at in places], axis=0)
        kv_places = [(s, at + Q_ROWS) for s, at in places]
        fresh = [got[s, at : at + KV_ROWS, :].astype(F32) for s, at in kv_places]
        mine = rows.at[at]
        mine[...] = jnp.concatenate(fresh, axis=0)
        new_keys = mine[pl.ds(0, 32, stride=2), :].astype(BF16)
        new_values = mine[pl.ds(1, 32, stride=2), :].astype(BF16)
        new_values = jnp.concatenate([new_values, jnp.ones((32, 128), BF16)], axis=1)
        scores = transposed_dot(queries, keys[...])
        reply = jnp.where(seen, transposed_dot(queries, new_keys), NEGATIVE)
        highest = jnp.maximum(
            jnp.max(scores, axis=1, keepdims=True), jnp.max(reply, axis=1, keepdims=True)
        )
        weights = jnp.exp2((scores - highest) * factor).astype(BF16)
        reply_weights = jnp.exp2((reply - highest) * factor).astype(BF16)
        summed = jnp.dot(weights, values[...], preferred_element_type=F32)
        summed = summed + jnp.dot(reply_weights, new_values, preferred_element_type=F32)
        attended = summed[:, 0:128] / summed[:, 128:256]
        for i in range(2 * CAP):
            one = unfold(attended[64 * i : 64 * i + 64], 8)
            attn_rows[at, i // CAP, i % CAP] = one.astype(BF16)

    def send_attended(at):
        target = back.at[pl.ds(2 * at, 2), :, :, pl.ds(channels, attn_rows.shape[4])]
        outs.append(pltpu.make_async_copy(attn_rows.at[at], target, sems_out.at[2 + at]))
        outs[-1].start()

    blocks = attn_rows.shape[0]
    for at in range(blocks // 2):
        attend(at)
    loads[2].wait()
    for at in range(0, channels, 256):
        part = state[at : at + 256, :]
        high = part.astype(BF16)
        low = (part - high.astype(F32)).astype(BF16)
        read = transposed_dot(c_hi, high) + transposed_dot(c_lo, high) + transposed_dot(c_hi, low)
        read_rows[:, :, :, at : at + 256] = read.astype(BF16).reshape(senders, CAP, 8, 256)
    outs.append(
        pltpu.make_async_copy(read_rows, back.at[:, :, :, pl.ds(0, channels)], sems_out.at[1])
    )
    outs[-1].start()
    for at in range(blocks // 2):
        send_attended(at)
    for at in range(blocks // 2, blocks):
        attend(at)
    for at in range(blocks // 2, blocks):
        send_attended(at)
    for copy in outs:
        copy.wait()


def to_channels(at, count, heads):
    head = at // 64 + lax.broadcasted_iota(jnp.int32, (128, count), 1) // 64
    source_head = lax.broadcasted_iota(jnp.int32, (128, count), 0) % heads
    return (head == source_head).astype(BF16)


def child_kernel(
    fork, old_rows_hbm, reply_x, bc, dt, kernel_x, kernel_bc, params,
    within, fade, old_rows, history, weights, rows_bc, sem,
):
    load = pltpu.make_async_copy(old_rows_hbm.at[pl.ds(0, old_rows.shape[0])], old_rows, sem)
    load.start()
    load.wait()
    children = reply_x.shape[0]
    count = children * 8
    for child in range(children):
        own = unfold(old_rows[fork[child]].astype(F32)[0:60], 3)
        history[8 * child : 8 * child + 8, :] = jnp.concatenate(
            [own, jnp.zeros((5, own.shape[1]), F32)], axis=0
        )

    def convolve(raw, old, taps):
        token = lax.broadcasted_iota(jnp.int32, raw.shape, 0) % 8
        total = raw * taps[3]
        for lag in range(1, 4):
            early = old if lag == 3 else pltpu.roll(old, count - (3 - lag), 0)
            joined = jnp.where(token < lag, early, pltpu.roll(raw, lag, 0))
            total = total + joined * taps[3 - lag]
        return silu(total)

    rows_bc[...] = bc[...].astype(F32).reshape(rows_bc.shape)
    channels = reply_x.shape[2]
    state = 256
    mats = []
    for part in range(2):
        raw = jnp.concatenate(bc_rows(rows_bc, part, 0, count), axis=1)
        at = channels + part * state
        taps = [kernel_bc[tap][part : part + 1] for tap in range(4)]
        mats.append(convolve(raw, history[:, at : at + state], taps))
    bmat = mats[0].reshape(children, 8, state)
    cmat = mats[1].reshape(children, 8, state)

    heads = dt.shape[2]
    spread = lax.broadcasted_iota(jnp.int32, (heads, 128), 1) % heads
    spread = (spread == lax.broadcasted_iota(jnp.int32, (heads, 128), 0)).astype(BF16)
    raw_dt = jnp.dot(
        dt[...].astype(F32).reshape(count, heads).astype(BF16), spread, preferred_element_type=F32
    )
    shifted = raw_dt + params[1:2]
    step_size = jnp.maximum(shifted, 0.0) + jnp.log1p(jnp.exp(-jnp.abs(shifted)))
    running = step_size * -jnp.exp(params[0:1])
    token = lax.broadcasted_iota(jnp.int32, (count, 128), 0) % 8
    for hop in (1, 2, 4):
        running = running + jnp.where(token >= hop, pltpu.roll(running, hop, 0), 0.0)
    lane = lax.broadcasted_iota(jnp.int32, (count, 128), 1) // heads

    def split(value):
        high = value.astype(BF16).astype(F32)
        rest = value - high
        middle = rest.astype(BF16).astype(F32)
        low = rest - middle
        parts = jnp.where(lane == 0, high, jnp.where(lane == 1, middle, jnp.where(lane == 2, low, 0.0)))
        return parts.astype(BF16)

    token3 = lax.broadcasted_iota(jnp.int32, (children, 8, 128), 1)
    running3 = running.reshape(children, 8, 128)
    step3 = step_size.reshape(children, 8, 128)
    skip = params[2:3][None]
    for source in range(8):
        overlap = jnp.sum(cmat * bmat[:, source : source + 1, :], axis=2, keepdims=True)
        later = token3 >= source
        span = jnp.where(later, running3 - running3[:, source : source + 1, :], 0.0)
        value = jnp.where(later, jnp.exp(span) * step3[:, source : source + 1, :] * overlap, 0.0)
        value = value + jnp.where(token3 == source, skip, 0.0)
        weights[source * count : (source + 1) * count, :] = split(value.reshape(count, 128))
    fade[...] = split(jnp.exp(running))

    per = 256
    for at in range(0, channels, per):
        raw = reply_x[:, :, at : at + per].astype(F32).reshape(count, per)
        taps = [kernel_x[tap : tap + 1, at : at + per] for tap in range(4)]
        xconv = convolve(raw, history[:, at : at + per], taps).reshape(children, 8, per)
        wide = jnp.dot(weights[...], to_channels(at, per, heads), preferred_element_type=F32)
        total = None
        for source in range(8):
            weight = wide[source * count : (source + 1) * count].reshape(children, 8, per)
            term = weight * xconv[:, source : source + 1, :]
            total = term if total is None else total + term
        within[:, :, at : at + per] = total


def finish_kernel(
    fork_any, lengths_any, got, gain, fade, within, gate, mamba, attn,
    count, fork, lengths, wide, mamba_rows, attn_rows, sems, sems_out,
):
    loads = [
        pltpu.make_async_copy(fork_any, fork, sems.at[0]),
        pltpu.make_async_copy(lengths_any, lengths, sems.at[1]),
    ]
    for load in loads:
        load.start()
    clear(count)
    children, _, channels = within.shape
    heads = channels // 64
    for at in range(0, channels, 256):
        some = jnp.dot(fade[...], to_channels(at, 256, heads), preferred_element_type=F32)
        wide[:, :, at : at + 256] = some.reshape(children, 8, 256)
    for load in loads:
        load.wait()
    per = 4
    token = lax.broadcasted_iota(jnp.int32, (8, 1), 0)
    places = [place_of(fork, count, child) for child in range(children)]
    outs = []
    for at in range(children // per):
        for child in range(per * at, per * at + per):
            parent, rank = places[child]
            read = got[parent, rank].astype(F32)
            mixer = wide[child] * read[:, 0:channels] + within[child]
            gated = mixer.astype(BF16).astype(F32) * silu(gate[child].astype(F32))
            meansq = jnp.mean(gated * gated, axis=1, keepdims=True)
            normed = gated * lax.rsqrt(meansq + EPSILON) * gain[...]
            valid = token < lengths[child]
            mamba_rows[child] = jnp.where(valid, normed, 0.0).astype(BF16)
            attn_rows[child] = jnp.where(valid, read[:, channels:], 0.0).astype(BF16)
        part = pl.ds(per * at, per)
        for i, (rows, out) in enumerate(((mamba_rows, mamba), (attn_rows, attn))):
            outs.append(pltpu.make_async_copy(rows.at[part], out.at[part], sems_out.at[i, at]))
            outs[-1].start()
    for copy in outs:
        copy.wait()


def params_of(mebibytes, flops, bytes_accessed, transcendentals=0):
    return dict(
        compiler_params=pltpu.CompilerParams(vmem_limit_bytes=mebibytes * 1024 * 1024),
        cost_estimate=pl.CostEstimate(
            flops=flops, bytes_accessed=bytes_accessed, transcendentals=transcendentals
        ),
    )


def local(
    reply_x,
    reply_bc,
    reply_dt,
    reply_gate,
    reply_query,
    reply_kv,
    lengths,
    fork_list,
    ssm_state,
    conv_x,
    conv_bc,
    kv_pool,
    page_table,
    kernel_x,
    kernel_bc,
    a_log,
    dt_bias,
    d_skip,
    norm_gain,
):
    children, tokens, channels = reply_x.shape
    siblings = lax.axis_size("sibling")
    state = ssm_state.shape[3]
    widths = reply_query.shape[2]
    heads = a_log.shape[0]
    fork = fork_list.reshape(children)
    news = reply_kv.reshape(children, 2 * tokens, AHDIM)
    halves = state // 128
    bc = reply_bc.reshape(children, tokens, 2, halves, 128).transpose(0, 1, 3, 2, 4)
    bc = bc.reshape(children, tokens * 2 * halves, 128)
    pool = kv_pool.reshape(kv_pool.shape[0], 256, AHDIM)
    flat_state = ssm_state.reshape(channels, state)
    params = jnp.tile(jnp.stack([a_log, dt_bias, d_skip]), (1, 128 // heads))
    gain = norm_gain.reshape(1, channels)
    rows_bc = pltpu.VMEM((bc.shape[0] * bc.shape[1], 128), F32)

    sources = (bc, conv_x, conv_bc, fork, reply_query, news)
    fork_held = pltpu.SMEM(fork.shape, fork.dtype)
    held = [pltpu.VMEM(source.shape, source.dtype) for source in sources]
    held[3] = fork_held
    send = pl.pallas_call(
        pack_kernel,
        out_shape=jax.ShapeDtypeStruct((siblings, SEND_ROWS, 128), BF16),
        in_specs=[whole(pltpu.HBM)] * 6,
        out_specs=whole(),
        scratch_shapes=[pltpu.SMEM((siblings,), jnp.int32)]
        + held
        + [pltpu.SemaphoreType.DMA((6,)), rows_bc],
        **params_of(60, 1_000_000, 2_000_000),
    )(*sources)
    got = lax.all_to_all(send, "sibling", split_axis=0, concat_axis=0, tiled=True)

    pages = page_table.shape[1]
    prefix = pl.pallas_call(
        prefix_kernel,
        out_shape=jax.ShapeDtypeStruct((PREFIX_ARRAYS, pages * 128, AHDIM), BF16),
        grid_spec=pltpu.PrefetchScalarGridSpec(
            num_scalar_prefetch=1,
            grid=(pages,),
            in_specs=[pl.BlockSpec((1, 256, AHDIM), lambda i, table: (table[0, i], 0, 0))],
            out_specs=pl.BlockSpec((2, 128, AHDIM), lambda i, table: (0, i, 0)),
            scratch_shapes=[pltpu.VMEM((256, AHDIM), F32)],
        ),
        **params_of(60, 4_000_000, 8_000_000),
    )(page_table, pool)

    back, old_rows = pl.pallas_call(
        parent_kernel,
        out_shape=(
            jax.ShapeDtypeStruct((siblings, CAP, tokens, channels + widths), BF16),
            jax.ShapeDtypeStruct((HISTORY_ROOM, HIST_ROWS, 128), BF16),
        ),
        in_specs=[whole()] * 3 + [whole(pltpu.HBM)] * 2,
        out_specs=(whole(pltpu.HBM), whole(pltpu.HBM)),
        scratch_shapes=[
            pltpu.VMEM((pages * 128, AHDIM), BF16),
            pltpu.VMEM((pages * 128, 2 * AHDIM), BF16),
            pltpu.VMEM((channels, state), F32),
            pltpu.VMEM((siblings, CAP, tokens, channels), BF16),
            pltpu.VMEM((siblings // 2, 2, CAP, tokens, widths), BF16),
            pltpu.VMEM((siblings // 2, 64, AHDIM), F32),
            pltpu.SemaphoreType.DMA((3,)),
            pltpu.SemaphoreType.DMA((2 + siblings // 2,)),
        ],
        **params_of(50, 6_000_000_000, 8_000_000, 4_000_000),
    )(got, conv_bc, kernel_bc, prefix, flat_state)
    returned = lax.all_to_all(back, "sibling", split_axis=0, concat_axis=0, tiled=True)

    wide = jax.ShapeDtypeStruct((children, tokens, channels), F32)
    within, fade = pl.pallas_call(
        child_kernel,
        out_shape=(wide, jax.ShapeDtypeStruct((children * tokens, 128), BF16)),
        in_specs=[whole(pltpu.SMEM), whole(pltpu.HBM)] + [whole()] * 6,
        out_specs=(whole(), whole()),
        scratch_shapes=[
            pltpu.VMEM((siblings, HIST_ROWS, 128), BF16),
            pltpu.VMEM((children * tokens, channels + 2 * state), F32),
            pltpu.VMEM((8 * children * tokens, 128), BF16),
            rows_bc,
            pltpu.SemaphoreType.DMA,
        ],
        **params_of(44, 600_000_000, 8_000_000, 1_000_000),
    )(fork, old_rows, reply_x, bc, reply_dt, kernel_x, kernel_bc, params)

    mamba = jax.ShapeDtypeStruct((children, tokens, channels), BF16)
    attn = jax.ShapeDtypeStruct((children, tokens, widths), BF16)
    return pl.pallas_call(
        finish_kernel,
        out_shape=(mamba, attn),
        in_specs=[whole(pl.ANY)] * 2 + [whole()] * 5,
        out_specs=(whole(pltpu.HBM), whole(pltpu.HBM)),
        scratch_shapes=[
            pltpu.SMEM((siblings,), jnp.int32),
            fork_held,
            fork_held,
            pltpu.VMEM(wide.shape, F32),
            pltpu.VMEM(mamba.shape, BF16),
            pltpu.VMEM(attn.shape, BF16),
            pltpu.SemaphoreType.DMA((2,)),
            pltpu.SemaphoreType.DMA((2, 4)),
        ],
        **params_of(40, 10_000_000, 6_000_000),
    )(fork, lengths, returned, gain, fade, within, reply_gate)


def solution(mesh):
    return jax.shard_map(
        local,
        mesh=mesh,
        in_specs=(
            P(("replica", "sibling"), None, "tensor"),
            P(("replica", "sibling"), None, None, "tensor"),
            P(("replica", "sibling"), None, "tensor"),
            P(("replica", "sibling"), None, "tensor"),
            P(("replica", "sibling"), None, "tensor"),
            P(("replica", "sibling"), None, None, "tensor"),
            P(("replica", "sibling")),
            P(("replica", "sibling"), None),
            P(("replica", "sibling"), "tensor", None, None),
            P(("replica", "sibling"), None, "tensor"),
            P(("replica", "sibling"), None, None, "tensor"),
            P(("replica", "sibling"), None, None, "tensor"),
            P(("replica", "sibling"), None),
            P(None, "tensor"),
            P(None, None, "tensor"),
            P("tensor"),
            P("tensor"),
            P("tensor"),
            P("tensor"),
        ),
        out_specs=(
            P(("replica", "sibling"), None, "tensor"),
            P(("replica", "sibling"), None, "tensor"),
        ),
        check_vma=False,
    )
```

```python
import math

import jax
import jax.numpy as jnp
from jax import lax
from jax.experimental import pallas as pl
from jax.experimental.pallas import tpu as pltpu
from jax.sharding import PartitionSpec as P

AHDIM = 128
CAP = 2
PREFIX_ARRAYS = 32
HISTORY_ROOM = 1024
GATE_ROOM = 512
NEGATIVE = -1e30
EPSILON = 1e-05
F32 = jnp.float32
BF16 = jnp.bfloat16

Q_ROWS = 64
KV_ROWS = 16
C_ROWS = 16
SLOT_ROWS = Q_ROWS + KV_ROWS + C_ROWS
HIST_AT = CAP * SLOT_ROWS
HIST_ROWS = 64
SEND_ROWS = HIST_AT + HIST_ROWS


def whole(memory_space=pltpu.VMEM):
    return pl.BlockSpec(memory_space=memory_space)


def silu(v):
    return v / (1.0 + jnp.exp(-v))


def fold(x, rows):
    return jnp.concatenate([x[:, i : i + 128] for i in range(0, x.shape[1], 128)], axis=0)


def unfold(x, rows):
    return jnp.concatenate([x[i : i + rows] for i in range(0, x.shape[0], rows)], axis=1)


def place_of(fork, count, child):
    parent = fork[child]
    rank = jnp.minimum(count[parent], CAP - 1)
    count[parent] = count[parent] + 1
    return parent, rank


def clear(count):
    for parent in range(count.shape[0]):
        count[parent] = 0


def bc_rows(rows_bc, part, at, count):
    start = 4 * at + part
    return [rows_bc[pl.ds(start + 2 * half, count, stride=4), :] for half in range(2)]


def pack_kernel(*refs):
    sources, (send, count), held, (sems, rows_bc) = refs[:6], refs[6:8], refs[8:14], refs[14:]
    copies = [
        pltpu.make_async_copy(source, kept, sems.at[i])
        for i, (source, kept) in enumerate(zip(sources, held))
    ]
    for copy in copies:
        copy.start()
    bc, conv_x, conv_bc, fork, query, news = held
    children = query.shape[0]
    clear(count)
    send[:, 0:HIST_AT, :] = jnp.zeros((send.shape[0], HIST_AT, 128), BF16)
    for copy in copies[:3]:
        copy.wait()
    rows_bc[...] = bc[...].astype(F32).reshape(rows_bc.shape)
    own_x = conv_x[0].astype(F32)
    pairs = [conv_bc[0, row].astype(F32) for row in range(3)]
    own_b = jnp.concatenate([pair[0:1] for pair in pairs], axis=0)
    own_c = jnp.concatenate([pair[1:2] for pair in pairs], axis=0)
    own = jnp.concatenate([own_x, own_b, own_c], axis=1)
    history = jnp.concatenate([fold(own, 3), jnp.zeros((4, 128), F32)], axis=0).astype(BF16)
    for parent in range(send.shape[0]):
        send[parent, HIST_AT:SEND_ROWS, :] = history
    for copy in copies[3:]:
        copy.wait()
    for child in range(children):
        parent, rank = place_of(fork, count, child)
        rows_q = fold(query[child].astype(F32), 8).astype(BF16)
        rows_c = jnp.concatenate(bc_rows(rows_bc, 1, 8 * child, 8), axis=0).astype(BF16)
        block = jnp.concatenate([rows_q, news[child], rows_c], axis=0)
        send[parent, pl.ds(pl.multiple_of(rank * SLOT_ROWS, 32), SLOT_ROWS), :] = block


def prefix_kernel(table, page, prefix, rows):
    rows[...] = page[0].astype(F32)
    for part in range(2):
        prefix[part] = rows[pl.ds(part, 128, stride=2), :].astype(BF16)


def transposed_dot(a, b):
    return lax.dot_general(a, b, (((1,), (1,)), ((), ())), preferred_element_type=F32)


def parent_kernel(
    got, conv_bc, kernel_bc, prefix_hbm, state_hbm, back, history,
    keys, values, state, read_rows, attn_rows, rows, sems, sems_out,
):
    senders = got.shape[0]
    pairs = [
        (prefix_hbm.at[0], keys),
        (prefix_hbm.at[1], values.at[:, pl.ds(0, 128)]),
        (state_hbm, state),
    ]
    loads = [pltpu.make_async_copy(*pair, sems.at[i]) for i, pair in enumerate(pairs)]
    for load in loads:
        load.start()
    old_rows = got.at[:, pl.ds(HIST_AT, HIST_ROWS), :]
    outs = [pltpu.make_async_copy(old_rows, history.at[pl.ds(0, senders)], sems_out.at[0])]
    outs[0].start()
    values[:, 128:256] = jnp.ones((values.shape[0], 128), BF16)
    raw = []
    for slot in range(CAP):
        at = slot * SLOT_ROWS + Q_ROWS + KV_ROWS
        part = got[:, at : at + C_ROWS, :].astype(F32)
        raw.append(jnp.concatenate([part[:, 0:8], part[:, 8:16]], axis=2))
    raw = jnp.concatenate(raw, axis=1).reshape(senders * CAP * 8, 256)
    old = [conv_bc[0, row].astype(F32)[1:2] for row in range(3)]
    token = lax.broadcasted_iota(jnp.int32, (senders * CAP, 8, 256), 1)
    taps = [kernel_bc[tap][1:2] for tap in range(4)]
    total = raw * taps[3]
    for lag in range(1, 4):
        early = jnp.concatenate(old[3 - lag :] + [jnp.zeros((8 - lag, 256), F32)], axis=0)
        moved = pltpu.roll(raw, lag, 0).reshape(senders * CAP, 8, 256)
        joined = jnp.where(token < lag, early[None], moved).reshape(raw.shape)
        total = total + joined * taps[3 - lag]
    cmat = silu(total)
    c_hi = cmat.astype(BF16)
    c_lo = (cmat - c_hi.astype(F32)).astype(BF16)
    channels = state.shape[0]

    factor = AHDIM**-0.5 * math.log2(math.e)
    row_ids = lax.broadcasted_iota(jnp.int32, (256, 32), 0)
    col_ids = lax.broadcasted_iota(jnp.int32, (256, 32), 1)
    seen = jnp.logical_and(row_ids // 64 == col_ids // 8, row_ids % 8 >= col_ids % 8)

    def prepare(at):
        sender = 2 * at
        places = [(sender + i, slot * SLOT_ROWS) for i in range(2) for slot in range(CAP)]
        queries = jnp.concatenate([got[s, at : at + Q_ROWS, :] for s, at in places], axis=0)
        kv_places = [(s, at + Q_ROWS) for s, at in places]
        fresh = [got[s, at : at + KV_ROWS, :].astype(F32) for s, at in kv_places]
        mine = rows.at[at]
        mine[...] = jnp.concatenate(fresh, axis=0)
        new_keys = mine[pl.ds(0, 32, stride=2), :].astype(BF16)
        new_values = mine[pl.ds(1, 32, stride=2), :].astype(BF16)
        new_values = jnp.concatenate([new_values, jnp.ones((32, 128), BF16)], axis=1)
        reply = jnp.where(seen, transposed_dot(queries, new_keys), NEGATIVE)
        return queries, reply, jnp.max(reply, axis=1, keepdims=True), new_values

    def attend(at, queries, reply, reply_highest, new_values):
        scores = transposed_dot(queries, keys[...])
        highest = jnp.maximum(jnp.max(scores, axis=1, keepdims=True), reply_highest)
        weights = jnp.exp2((scores - highest) * factor).astype(BF16)
        reply_weights = jnp.exp2((reply - highest) * factor).astype(BF16)
        summed = jnp.dot(weights, values[...], preferred_element_type=F32)
        summed = summed + jnp.dot(reply_weights, new_values, preferred_element_type=F32)
        attended = summed[:, 0:128] / summed[:, 128:256]
        for i in range(2 * CAP):
            one = unfold(attended[64 * i : 64 * i + 64], 8)
            attn_rows[at, i // CAP, i % CAP] = one.astype(BF16)

    def send_attended(at):
        target = back.at[pl.ds(2 * at, 2), :, :, pl.ds(channels, attn_rows.shape[4])]
        outs.append(pltpu.make_async_copy(attn_rows.at[at], target, sems_out.at[2 + at]))
        outs[-1].start()

    blocks = attn_rows.shape[0]
    ready = [prepare(at) for at in range(blocks)]
    for load in loads[0:2]:
        load.wait()
    for at in range(blocks // 2):
        attend(at, *ready[at])
    loads[2].wait()
    for at in range(0, channels, 256):
        part = state[at : at + 256, :]
        high = part.astype(BF16)
        low = (part - high.astype(F32)).astype(BF16)
        read = transposed_dot(c_hi, high) + transposed_dot(c_lo, high) + transposed_dot(c_hi, low)
        read_rows[:, :, :, at : at + 256] = read.astype(BF16).reshape(senders, CAP, 8, 256)
    outs.append(
        pltpu.make_async_copy(read_rows, back.at[:, :, :, pl.ds(0, channels)], sems_out.at[1])
    )
    outs[-1].start()
    for at in range(blocks // 2):
        send_attended(at)
    for at in range(blocks // 2, blocks):
        attend(at, *ready[at])
    for at in range(blocks // 2, blocks):
        send_attended(at)
    for copy in outs:
        copy.wait()


def to_channels(at, count, heads):
    head = at // 64 + lax.broadcasted_iota(jnp.int32, (128, count), 1) // 64
    source_head = lax.broadcasted_iota(jnp.int32, (128, count), 0) % heads
    return (head == source_head).astype(BF16)


def child_kernel(
    fork, old_rows_hbm, reply_x, bc, dt, kernel_x, kernel_bc, params, gate,
    within, fade, kept_gate, old_rows, history, weights, rows_bc, sem, sem_gate,
):
    keep = pltpu.make_async_copy(gate, kept_gate.at[pl.ds(0, gate.shape[0])], sem_gate)
    keep.start()
    load = pltpu.make_async_copy(old_rows_hbm.at[pl.ds(0, old_rows.shape[0])], old_rows, sem)
    load.start()
    load.wait()
    children = reply_x.shape[0]
    count = children * 8
    for child in range(children):
        own = unfold(old_rows[fork[child]].astype(F32)[0:60], 3)
        history[8 * child : 8 * child + 8, :] = jnp.concatenate(
            [own, jnp.zeros((5, own.shape[1]), F32)], axis=0
        )

    def convolve(raw, old, taps):
        token = lax.broadcasted_iota(jnp.int32, raw.shape, 0) % 8
        total = raw * taps[3]
        for lag in range(1, 4):
            early = old if lag == 3 else pltpu.roll(old, count - (3 - lag), 0)
            joined = jnp.where(token < lag, early, pltpu.roll(raw, lag, 0))
            total = total + joined * taps[3 - lag]
        return silu(total)

    rows_bc[...] = bc[...].astype(F32).reshape(rows_bc.shape)
    channels = reply_x.shape[2]
    state = 256
    mats = []
    for part in range(2):
        raw = jnp.concatenate(bc_rows(rows_bc, part, 0, count), axis=1)
        at = channels + part * state
        taps = [kernel_bc[tap][part : part + 1] for tap in range(4)]
        mats.append(convolve(raw, history[:, at : at + state], taps))
    bmat = mats[0].reshape(children, 8, state)
    cmat = mats[1].reshape(children, 8, state)

    heads = dt.shape[2]
    spread = lax.broadcasted_iota(jnp.int32, (heads, 128), 1) % heads
    spread = (spread == lax.broadcasted_iota(jnp.int32, (heads, 128), 0)).astype(BF16)
    raw_dt = jnp.dot(
        dt[...].astype(F32).reshape(count, heads).astype(BF16), spread, preferred_element_type=F32
    )
    shifted = raw_dt + params[1:2]
    step_size = jnp.maximum(shifted, 0.0) + jnp.log1p(jnp.exp(-jnp.abs(shifted)))
    running = step_size * -jnp.exp(params[0:1])
    token = lax.broadcasted_iota(jnp.int32, (count, 128), 0) % 8
    for hop in (1, 2, 4):
        running = running + jnp.where(token >= hop, pltpu.roll(running, hop, 0), 0.0)
    lane = lax.broadcasted_iota(jnp.int32, (count, 128), 1) // heads

    def split(value):
        high = value.astype(BF16).astype(F32)
        rest = value - high
        middle = rest.astype(BF16).astype(F32)
        low = rest - middle
        parts = jnp.where(lane == 0, high, jnp.where(lane == 1, middle, jnp.where(lane == 2, low, 0.0)))
        return parts.astype(BF16)

    token3 = lax.broadcasted_iota(jnp.int32, (children, 8, 128), 1)
    running3 = running.reshape(children, 8, 128)
    step3 = step_size.reshape(children, 8, 128)
    skip = params[2:3][None]
    for source in range(8):
        overlap = jnp.sum(cmat * bmat[:, source : source + 1, :], axis=2, keepdims=True)
        later = token3 >= source
        span = jnp.where(later, running3 - running3[:, source : source + 1, :], 0.0)
        value = jnp.where(later, jnp.exp(span) * step3[:, source : source + 1, :] * overlap, 0.0)
        value = value + jnp.where(token3 == source, skip, 0.0)
        weights[source * count : (source + 1) * count, :] = split(value.reshape(count, 128))
    fade[...] = split(jnp.exp(running))

    per = 256
    for at in range(0, channels, per):
        raw = reply_x[:, :, at : at + per].astype(F32).reshape(count, per)
        taps = [kernel_x[tap : tap + 1, at : at + per] for tap in range(4)]
        xconv = convolve(raw, history[:, at : at + per], taps).reshape(children, 8, per)
        wide = jnp.dot(weights[...], to_channels(at, per, heads), preferred_element_type=F32)
        total = None
        for source in range(8):
            weight = wide[source * count : (source + 1) * count].reshape(children, 8, per)
            term = weight * xconv[:, source : source + 1, :]
            total = term if total is None else total + term
        within[:, :, at : at + per] = total
    keep.wait()


def finish_kernel(
    fork_any, lengths_any, got, gain, fade, within, gate_hbm, mamba, attn,
    count, fork, lengths, gate, wide, mamba_rows, attn_rows, sems, sems_out,
):
    loads = [
        pltpu.make_async_copy(fork_any, fork, sems.at[0]),
        pltpu.make_async_copy(lengths_any, lengths, sems.at[1]),
        pltpu.make_async_copy(gate_hbm.at[pl.ds(0, gate.shape[0])], gate, sems.at[2]),
    ]
    for load in loads:
        load.start()
    clear(count)
    children, _, channels = within.shape
    heads = channels // 64
    for at in range(0, channels, 256):
        some = jnp.dot(fade[...], to_channels(at, 256, heads), preferred_element_type=F32)
        wide[:, :, at : at + 256] = some.reshape(children, 8, 256)
    for load in loads:
        load.wait()
    per = 4
    token = lax.broadcasted_iota(jnp.int32, (8, 1), 0)
    places = [place_of(fork, count, child) for child in range(children)]
    outs = []
    for at in range(children // per):
        for child in range(per * at, per * at + per):
            parent, rank = places[child]
            read = got[parent, rank].astype(F32)
            mixer = wide[child] * read[:, 0:channels] + within[child]
            gated = mixer.astype(BF16).astype(F32) * silu(gate[child].astype(F32))
            meansq = jnp.mean(gated * gated, axis=1, keepdims=True)
            normed = gated * lax.rsqrt(meansq + EPSILON) * gain[...]
            valid = token < lengths[child]
            mamba_rows[child] = jnp.where(valid, normed, 0.0).astype(BF16)
            attn_rows[child] = jnp.where(valid, read[:, channels:], 0.0).astype(BF16)
        part = pl.ds(per * at, per)
        for i, (rows, out) in enumerate(((mamba_rows, mamba), (attn_rows, attn))):
            outs.append(pltpu.make_async_copy(rows.at[part], out.at[part], sems_out.at[i, at]))
            outs[-1].start()
    for copy in outs:
        copy.wait()


def params_of(mebibytes, flops, bytes_accessed, transcendentals=0):
    return dict(
        compiler_params=pltpu.CompilerParams(vmem_limit_bytes=mebibytes * 1024 * 1024),
        cost_estimate=pl.CostEstimate(
            flops=flops, bytes_accessed=bytes_accessed, transcendentals=transcendentals
        ),
    )


def local(
    reply_x,
    reply_bc,
    reply_dt,
    reply_gate,
    reply_query,
    reply_kv,
    lengths,
    fork_list,
    ssm_state,
    conv_x,
    conv_bc,
    kv_pool,
    page_table,
    kernel_x,
    kernel_bc,
    a_log,
    dt_bias,
    d_skip,
    norm_gain,
):
    children, tokens, channels = reply_x.shape
    siblings = lax.axis_size("sibling")
    state = ssm_state.shape[3]
    widths = reply_query.shape[2]
    heads = a_log.shape[0]
    fork = fork_list.reshape(children)
    news = reply_kv.reshape(children, 2 * tokens, AHDIM)
    halves = state // 128
    bc = reply_bc.reshape(children, tokens, 2, halves, 128).transpose(0, 1, 3, 2, 4)
    bc = bc.reshape(children, tokens * 2 * halves, 128)
    pool = kv_pool.reshape(kv_pool.shape[0], 256, AHDIM)
    flat_state = ssm_state.reshape(channels, state)
    params = jnp.tile(jnp.stack([a_log, dt_bias, d_skip]), (1, 128 // heads))
    gain = norm_gain.reshape(1, channels)
    rows_bc = pltpu.VMEM((bc.shape[0] * bc.shape[1], 128), F32)

    sources = (bc, conv_x, conv_bc, fork, reply_query, news)
    fork_held = pltpu.SMEM(fork.shape, fork.dtype)
    held = [pltpu.VMEM(source.shape, source.dtype) for source in sources]
    held[3] = fork_held
    send = pl.pallas_call(
        pack_kernel,
        out_shape=jax.ShapeDtypeStruct((siblings, SEND_ROWS, 128), BF16),
        in_specs=[whole(pltpu.HBM)] * 6,
        out_specs=whole(),
        scratch_shapes=[pltpu.SMEM((siblings,), jnp.int32)]
        + held
        + [pltpu.SemaphoreType.DMA((6,)), rows_bc],
        **params_of(60, 1_000_000, 2_000_000),
    )(*sources)
    got = lax.all_to_all(send, "sibling", split_axis=0, concat_axis=0, tiled=True)

    pages = page_table.shape[1]
    prefix = pl.pallas_call(
        prefix_kernel,
        out_shape=jax.ShapeDtypeStruct((PREFIX_ARRAYS, pages * 128, AHDIM), BF16),
        grid_spec=pltpu.PrefetchScalarGridSpec(
            num_scalar_prefetch=1,
            grid=(pages,),
            in_specs=[pl.BlockSpec((1, 256, AHDIM), lambda i, table: (table[0, i], 0, 0))],
            out_specs=pl.BlockSpec((2, 128, AHDIM), lambda i, table: (0, i, 0)),
            scratch_shapes=[pltpu.VMEM((256, AHDIM), F32)],
        ),
        **params_of(60, 4_000_000, 8_000_000),
    )(page_table, pool)

    back, old_rows = pl.pallas_call(
        parent_kernel,
        out_shape=(
            jax.ShapeDtypeStruct((siblings, CAP, tokens, channels + widths), BF16),
            jax.ShapeDtypeStruct((HISTORY_ROOM, HIST_ROWS, 128), BF16),
        ),
        in_specs=[whole()] * 3 + [whole(pltpu.HBM)] * 2,
        out_specs=(whole(pltpu.HBM), whole(pltpu.HBM)),
        scratch_shapes=[
            pltpu.VMEM((pages * 128, AHDIM), BF16),
            pltpu.VMEM((pages * 128, 2 * AHDIM), BF16),
            pltpu.VMEM((channels, state), F32),
            pltpu.VMEM((siblings, CAP, tokens, channels), BF16),
            pltpu.VMEM((siblings // 2, 2, CAP, tokens, widths), BF16),
            pltpu.VMEM((siblings // 2, 64, AHDIM), F32),
            pltpu.SemaphoreType.DMA((3,)),
            pltpu.SemaphoreType.DMA((2 + siblings // 2,)),
        ],
        **params_of(50, 6_000_000_000, 8_000_000, 4_000_000),
    )(got, conv_bc, kernel_bc, prefix, flat_state)
    returned = lax.all_to_all(back, "sibling", split_axis=0, concat_axis=0, tiled=True)

    wide = jax.ShapeDtypeStruct((children, tokens, channels), F32)
    within, fade, gate = pl.pallas_call(
        child_kernel,
        out_shape=(
            wide,
            jax.ShapeDtypeStruct((children * tokens, 128), BF16),
            jax.ShapeDtypeStruct((GATE_ROOM,) + reply_gate.shape[1:], BF16),
        ),
        in_specs=[whole(pltpu.SMEM), whole(pltpu.HBM)] + [whole()] * 6 + [whole(pltpu.HBM)],
        out_specs=(whole(), whole(), whole(pltpu.HBM)),
        scratch_shapes=[
            pltpu.VMEM((siblings, HIST_ROWS, 128), BF16),
            pltpu.VMEM((children * tokens, channels + 2 * state), F32),
            pltpu.VMEM((8 * children * tokens, 128), BF16),
            rows_bc,
            pltpu.SemaphoreType.DMA,
            pltpu.SemaphoreType.DMA,
        ],
        **params_of(44, 600_000_000, 8_000_000, 1_000_000),
    )(fork, old_rows, reply_x, bc, reply_dt, kernel_x, kernel_bc, params, reply_gate)

    mamba = jax.ShapeDtypeStruct((children, tokens, channels), BF16)
    attn = jax.ShapeDtypeStruct((children, tokens, widths), BF16)
    return pl.pallas_call(
        finish_kernel,
        out_shape=(mamba, attn),
        in_specs=[whole(pl.ANY)] * 2 + [whole()] * 4 + [whole(pltpu.HBM)],
        out_specs=(whole(pltpu.HBM), whole(pltpu.HBM)),
        scratch_shapes=[
            pltpu.SMEM((siblings,), jnp.int32),
            fork_held,
            fork_held,
            pltpu.VMEM(reply_gate.shape, BF16),
            pltpu.VMEM(wide.shape, F32),
            pltpu.VMEM(mamba.shape, BF16),
            pltpu.VMEM(attn.shape, BF16),
            pltpu.SemaphoreType.DMA((3,)),
            pltpu.SemaphoreType.DMA((2, 4)),
        ],
        **params_of(46, 10_000_000, 6_000_000),
    )(fork, lengths, returned, gain, fade, within, gate)


def solution(mesh):
    return jax.shard_map(
        local,
        mesh=mesh,
        in_specs=(
            P(("replica", "sibling"), None, "tensor"),
            P(("replica", "sibling"), None, None, "tensor"),
            P(("replica", "sibling"), None, "tensor"),
            P(("replica", "sibling"), None, "tensor"),
            P(("replica", "sibling"), None, "tensor"),
            P(("replica", "sibling"), None, None, "tensor"),
            P(("replica", "sibling")),
            P(("replica", "sibling"), None),
            P(("replica", "sibling"), "tensor", None, None),
            P(("replica", "sibling"), None, "tensor"),
            P(("replica", "sibling"), None, None, "tensor"),
            P(("replica", "sibling"), None, None, "tensor"),
            P(("replica", "sibling"), None),
            P(None, "tensor"),
            P(None, None, "tensor"),
            P("tensor"),
            P("tensor"),
            P("tensor"),
            P("tensor"),
        ),
        out_specs=(
            P(("replica", "sibling"), None, "tensor"),
            P(("replica", "sibling"), None, "tensor"),
        ),
        check_vma=False,
    )
```

```python
import math

import jax
import jax.numpy as jnp
from jax import lax
from jax.experimental import pallas as pl
from jax.experimental.pallas import tpu as pltpu
from jax.sharding import PartitionSpec as P

AHDIM = 128
CAP = 2
PREFIX_ARRAYS = 32
HISTORY_ROOM = 1024
GATE_ROOM = 512
NEGATIVE = -1e30
EPSILON = 1e-05
F32 = jnp.float32
BF16 = jnp.bfloat16

Q_ROWS = 64
KV_ROWS = 16
C_ROWS = 16
SLOT_ROWS = Q_ROWS + KV_ROWS + C_ROWS
HIST_AT = CAP * SLOT_ROWS
HIST_ROWS = 64
SEND_ROWS = HIST_AT + HIST_ROWS


def whole(memory_space=pltpu.VMEM):
    return pl.BlockSpec(memory_space=memory_space)


def silu(v):
    return v / (1.0 + jnp.exp(-v))


def fold(x, rows):
    return jnp.concatenate([x[:, i : i + 128] for i in range(0, x.shape[1], 128)], axis=0)


def unfold(x, rows):
    return jnp.concatenate([x[i : i + rows] for i in range(0, x.shape[0], rows)], axis=1)


def place_of(fork, count, child):
    parent = fork[child]
    rank = jnp.minimum(count[parent], CAP - 1)
    count[parent] = count[parent] + 1
    return parent, rank


def clear(count):
    for parent in range(count.shape[0]):
        count[parent] = 0


def bc_rows(rows_bc, part, at, count):
    start = 4 * at + part
    return [rows_bc[pl.ds(start + 2 * half, count, stride=4), :] for half in range(2)]


def pack_kernel(*refs):
    sources, (send, count), held, (sems, rows_bc) = refs[:6], refs[6:8], refs[8:14], refs[14:]
    copies = [
        pltpu.make_async_copy(source, kept, sems.at[i])
        for i, (source, kept) in enumerate(zip(sources, held))
    ]
    for copy in copies:
        copy.start()
    bc, conv_x, conv_bc, fork, query, news = held
    children = query.shape[0]
    clear(count)
    send[:, 0:HIST_AT, :] = jnp.zeros((send.shape[0], HIST_AT, 128), BF16)
    for copy in copies[:3]:
        copy.wait()
    rows_bc[...] = bc[...].astype(F32).reshape(rows_bc.shape)
    own_x = conv_x[0].astype(F32)
    pairs = [conv_bc[0, row].astype(F32) for row in range(3)]
    own_b = jnp.concatenate([pair[0:1] for pair in pairs], axis=0)
    own_c = jnp.concatenate([pair[1:2] for pair in pairs], axis=0)
    own = jnp.concatenate([own_x, own_b, own_c], axis=1)
    history = jnp.concatenate([fold(own, 3), jnp.zeros((4, 128), F32)], axis=0).astype(BF16)
    for parent in range(send.shape[0]):
        send[parent, HIST_AT:SEND_ROWS, :] = history
    for copy in copies[3:]:
        copy.wait()
    for child in range(children):
        parent, rank = place_of(fork, count, child)
        rows_q = fold(query[child].astype(F32), 8).astype(BF16)
        rows_c = jnp.concatenate(bc_rows(rows_bc, 1, 8 * child, 8), axis=0).astype(BF16)
        block = jnp.concatenate([rows_q, news[child], rows_c], axis=0)
        send[parent, pl.ds(pl.multiple_of(rank * SLOT_ROWS, 32), SLOT_ROWS), :] = block


def prefix_kernel(table, page, prefix, rows):
    rows[...] = page[0].astype(F32)
    for part in range(2):
        prefix[part] = rows[pl.ds(part, 128, stride=2), :].astype(BF16)


def transposed_dot(a, b):
    return lax.dot_general(a, b, (((1,), (1,)), ((), ())), preferred_element_type=F32)


def parent_kernel(
    got, conv_bc, kernel_bc, prefix_hbm, state_hbm, back, history,
    keys, values, state, read_rows, attn_rows, rows, sems, sems_out,
):
    senders = got.shape[0]
    pairs = [
        (prefix_hbm.at[0], keys),
        (prefix_hbm.at[1], values.at[:, pl.ds(0, 128)]),
        (state_hbm, state),
    ]
    loads = [pltpu.make_async_copy(*pair, sems.at[i]) for i, pair in enumerate(pairs)]
    for load in loads:
        load.start()
    old_rows = got.at[:, pl.ds(HIST_AT, HIST_ROWS), :]
    outs = [pltpu.make_async_copy(old_rows, history.at[pl.ds(0, senders)], sems_out.at[0])]
    outs[0].start()
    values[:, 128:256] = jnp.ones((values.shape[0], 128), BF16)
    raw = []
    for slot in range(CAP):
        at = slot * SLOT_ROWS + Q_ROWS + KV_ROWS
        part = got[:, at : at + C_ROWS, :].astype(F32)
        raw.append(jnp.concatenate([part[:, 0:8], part[:, 8:16]], axis=2))
    raw = jnp.concatenate(raw, axis=1).reshape(senders * CAP * 8, 256)
    old = [conv_bc[0, row].astype(F32)[1:2] for row in range(3)]
    token = lax.broadcasted_iota(jnp.int32, (senders * CAP, 8, 256), 1)
    taps = [kernel_bc[tap][1:2] for tap in range(4)]
    total = raw * taps[3]
    for lag in range(1, 4):
        early = jnp.concatenate(old[3 - lag :] + [jnp.zeros((8 - lag, 256), F32)], axis=0)
        moved = pltpu.roll(raw, lag, 0).reshape(senders * CAP, 8, 256)
        joined = jnp.where(token < lag, early[None], moved).reshape(raw.shape)
        total = total + joined * taps[3 - lag]
    cmat = silu(total)
    cmat = cmat.astype(BF16)
    channels = state.shape[0]

    factor = AHDIM**-0.5 * math.log2(math.e)
    row_ids = lax.broadcasted_iota(jnp.int32, (256, 32), 0)
    col_ids = lax.broadcasted_iota(jnp.int32, (256, 32), 1)
    seen = jnp.logical_and(row_ids // 64 == col_ids // 8, row_ids % 8 >= col_ids % 8)

    def prepare(at):
        sender = 2 * at
        places = [(sender + i, slot * SLOT_ROWS) for i in range(2) for slot in range(CAP)]
        queries = jnp.concatenate([got[s, at : at + Q_ROWS, :] for s, at in places], axis=0)
        kv_places = [(s, at + Q_ROWS) for s, at in places]
        fresh = [got[s, at : at + KV_ROWS, :].astype(F32) for s, at in kv_places]
        mine = rows.at[at]
        mine[...] = jnp.concatenate(fresh, axis=0)
        new_keys = mine[pl.ds(0, 32, stride=2), :].astype(BF16)
        new_values = mine[pl.ds(1, 32, stride=2), :].astype(BF16)
        new_values = jnp.concatenate([new_values, jnp.ones((32, 128), BF16)], axis=1)
        reply = jnp.where(seen, transposed_dot(queries, new_keys), NEGATIVE)
        return queries, reply, jnp.max(reply, axis=1, keepdims=True), new_values

    def attend(at, queries, reply, reply_highest, new_values):
        scores = transposed_dot(queries, keys[...])
        highest = jnp.maximum(jnp.max(scores, axis=1, keepdims=True), reply_highest)
        weights = jnp.exp2((scores - highest) * factor).astype(BF16)
        reply_weights = jnp.exp2((reply - highest) * factor).astype(BF16)
        summed = jnp.dot(weights, values[...], preferred_element_type=F32)
        summed = summed + jnp.dot(reply_weights, new_values, preferred_element_type=F32)
        attended = summed[:, 0:128] / summed[:, 128:256]
        for i in range(2 * CAP):
            one = unfold(attended[64 * i : 64 * i + 64], 8)
            attn_rows[at, i // CAP, i % CAP] = one.astype(BF16)

    def send_attended(at):
        target = back.at[pl.ds(2 * at, 2), :, :, pl.ds(channels, attn_rows.shape[4])]
        outs.append(pltpu.make_async_copy(attn_rows.at[at], target, sems_out.at[2 + at]))
        outs[-1].start()

    blocks = attn_rows.shape[0]
    ready = [prepare(at) for at in range(blocks)]
    for load in loads[0:2]:
        load.wait()
    for at in range(blocks // 2):
        attend(at, *ready[at])
    loads[2].wait()
    for at in range(0, channels, 256):
        read = transposed_dot(cmat, state[at : at + 256, :].astype(BF16))
        read_rows[:, :, :, at : at + 256] = read.astype(BF16).reshape(senders, CAP, 8, 256)
    outs.append(
        pltpu.make_async_copy(read_rows, back.at[:, :, :, pl.ds(0, channels)], sems_out.at[1])
    )
    outs[-1].start()
    for at in range(blocks // 2):
        send_attended(at)
    for at in range(blocks // 2, blocks):
        attend(at, *ready[at])
    for at in range(blocks // 2, blocks):
        send_attended(at)
    for copy in outs:
        copy.wait()


def to_channels(at, count, heads):
    head = at // 64 + lax.broadcasted_iota(jnp.int32, (128, count), 1) // 64
    source_head = lax.broadcasted_iota(jnp.int32, (128, count), 0) % heads
    return (head == source_head).astype(BF16)


def child_kernel(
    fork, old_rows_hbm, reply_x, bc, dt, kernel_x, kernel_bc, params, gate,
    within, fade, kept_gate, old_rows, history, weights, rows_bc, sem, sem_gate,
):
    keep = pltpu.make_async_copy(gate, kept_gate.at[pl.ds(0, gate.shape[0])], sem_gate)
    keep.start()
    load = pltpu.make_async_copy(old_rows_hbm.at[pl.ds(0, old_rows.shape[0])], old_rows, sem)
    load.start()
    load.wait()
    children = reply_x.shape[0]
    count = children * 8
    for child in range(children):
        own = unfold(old_rows[fork[child]].astype(F32)[0:60], 3)
        history[8 * child : 8 * child + 8, :] = jnp.concatenate(
            [own, jnp.zeros((5, own.shape[1]), F32)], axis=0
        )

    def convolve(raw, old, taps):
        token = lax.broadcasted_iota(jnp.int32, raw.shape, 0) % 8
        total = raw * taps[3]
        for lag in range(1, 4):
            early = old if lag == 3 else pltpu.roll(old, count - (3 - lag), 0)
            joined = jnp.where(token < lag, early, pltpu.roll(raw, lag, 0))
            total = total + joined * taps[3 - lag]
        return silu(total)

    rows_bc[...] = bc[...].astype(F32).reshape(rows_bc.shape)
    channels = reply_x.shape[2]
    state = 256
    mats = []
    for part in range(2):
        raw = jnp.concatenate(bc_rows(rows_bc, part, 0, count), axis=1)
        at = channels + part * state
        taps = [kernel_bc[tap][part : part + 1] for tap in range(4)]
        mats.append(convolve(raw, history[:, at : at + state], taps))
    bmat = mats[0].reshape(children, 8, state)
    cmat = mats[1].reshape(children, 8, state)

    heads = dt.shape[2]
    spread = lax.broadcasted_iota(jnp.int32, (heads, 128), 1) % heads
    spread = (spread == lax.broadcasted_iota(jnp.int32, (heads, 128), 0)).astype(BF16)
    raw_dt = jnp.dot(
        dt[...].astype(F32).reshape(count, heads).astype(BF16), spread, preferred_element_type=F32
    )
    shifted = raw_dt + params[1:2]
    step_size = jnp.maximum(shifted, 0.0) + jnp.log1p(jnp.exp(-jnp.abs(shifted)))
    running = step_size * -jnp.exp(params[0:1])
    token = lax.broadcasted_iota(jnp.int32, (count, 128), 0) % 8
    for hop in (1, 2, 4):
        running = running + jnp.where(token >= hop, pltpu.roll(running, hop, 0), 0.0)
    lane = lax.broadcasted_iota(jnp.int32, (count, 128), 1) // heads

    def split(value):
        high = value.astype(BF16).astype(F32)
        rest = value - high
        middle = rest.astype(BF16).astype(F32)
        low = rest - middle
        parts = jnp.where(lane == 0, high, jnp.where(lane == 1, middle, jnp.where(lane == 2, low, 0.0)))
        return parts.astype(BF16)

    token3 = lax.broadcasted_iota(jnp.int32, (children, 8, 128), 1)
    running3 = running.reshape(children, 8, 128)
    step3 = step_size.reshape(children, 8, 128)
    skip = params[2:3][None]
    for source in range(8):
        overlap = jnp.sum(cmat * bmat[:, source : source + 1, :], axis=2, keepdims=True)
        later = token3 >= source
        span = jnp.where(later, running3 - running3[:, source : source + 1, :], 0.0)
        value = jnp.where(later, jnp.exp(span) * step3[:, source : source + 1, :] * overlap, 0.0)
        value = value + jnp.where(token3 == source, skip, 0.0)
        weights[source * count : (source + 1) * count, :] = split(value.reshape(count, 128))
    fade[...] = split(jnp.exp(running))

    per = 256
    for at in range(0, channels, per):
        raw = reply_x[:, :, at : at + per].astype(F32).reshape(count, per)
        taps = [kernel_x[tap : tap + 1, at : at + per] for tap in range(4)]
        xconv = convolve(raw, history[:, at : at + per], taps).reshape(children, 8, per)
        wide = jnp.dot(weights[...], to_channels(at, per, heads), preferred_element_type=F32)
        total = None
        for source in range(8):
            weight = wide[source * count : (source + 1) * count].reshape(children, 8, per)
            term = weight * xconv[:, source : source + 1, :]
            total = term if total is None else total + term
        within[:, :, at : at + per] = total
    keep.wait()


def finish_kernel(
    fork_any, lengths_any, got, gain, fade, within, gate_hbm, mamba, attn,
    count, fork, lengths, gate, wide, mamba_rows, attn_rows, sems, sems_out,
):
    loads = [
        pltpu.make_async_copy(fork_any, fork, sems.at[0]),
        pltpu.make_async_copy(lengths_any, lengths, sems.at[1]),
        pltpu.make_async_copy(gate_hbm.at[pl.ds(0, gate.shape[0])], gate, sems.at[2]),
    ]
    for load in loads:
        load.start()
    clear(count)
    children, _, channels = within.shape
    heads = channels // 64
    for at in range(0, channels, 256):
        some = jnp.dot(fade[...], to_channels(at, 256, heads), preferred_element_type=F32)
        wide[:, :, at : at + 256] = some.reshape(children, 8, 256)
    for load in loads:
        load.wait()
    per = 4
    token = lax.broadcasted_iota(jnp.int32, (8, 1), 0)
    places = [place_of(fork, count, child) for child in range(children)]
    outs = []
    for at in range(children // per):
        for child in range(per * at, per * at + per):
            parent, rank = places[child]
            read = got[parent, rank].astype(F32)
            mixer = wide[child] * read[:, 0:channels] + within[child]
            gated = mixer.astype(BF16).astype(F32) * silu(gate[child].astype(F32))
            meansq = jnp.mean(gated * gated, axis=1, keepdims=True)
            normed = gated * lax.rsqrt(meansq + EPSILON) * gain[...]
            valid = token < lengths[child]
            mamba_rows[child] = jnp.where(valid, normed, 0.0).astype(BF16)
            attn_rows[child] = jnp.where(valid, read[:, channels:], 0.0).astype(BF16)
        part = pl.ds(per * at, per)
        for i, (rows, out) in enumerate(((mamba_rows, mamba), (attn_rows, attn))):
            outs.append(pltpu.make_async_copy(rows.at[part], out.at[part], sems_out.at[i, at]))
            outs[-1].start()
    for copy in outs:
        copy.wait()


def params_of(mebibytes, flops, bytes_accessed, transcendentals=0):
    return dict(
        compiler_params=pltpu.CompilerParams(vmem_limit_bytes=mebibytes * 1024 * 1024),
        cost_estimate=pl.CostEstimate(
            flops=flops, bytes_accessed=bytes_accessed, transcendentals=transcendentals
        ),
    )


def local(
    reply_x,
    reply_bc,
    reply_dt,
    reply_gate,
    reply_query,
    reply_kv,
    lengths,
    fork_list,
    ssm_state,
    conv_x,
    conv_bc,
    kv_pool,
    page_table,
    kernel_x,
    kernel_bc,
    a_log,
    dt_bias,
    d_skip,
    norm_gain,
):
    children, tokens, channels = reply_x.shape
    siblings = lax.axis_size("sibling")
    state = ssm_state.shape[3]
    widths = reply_query.shape[2]
    heads = a_log.shape[0]
    fork = fork_list.reshape(children)
    news = reply_kv.reshape(children, 2 * tokens, AHDIM)
    halves = state // 128
    bc = reply_bc.reshape(children, tokens, 2, halves, 128).transpose(0, 1, 3, 2, 4)
    bc = bc.reshape(children, tokens * 2 * halves, 128)
    pool = kv_pool.reshape(kv_pool.shape[0], 256, AHDIM)
    flat_state = ssm_state.reshape(channels, state)
    params = jnp.tile(jnp.stack([a_log, dt_bias, d_skip]), (1, 128 // heads))
    gain = norm_gain.reshape(1, channels)
    rows_bc = pltpu.VMEM((bc.shape[0] * bc.shape[1], 128), F32)

    sources = (bc, conv_x, conv_bc, fork, reply_query, news)
    fork_held = pltpu.SMEM(fork.shape, fork.dtype)
    held = [pltpu.VMEM(source.shape, source.dtype) for source in sources]
    held[3] = fork_held
    send = pl.pallas_call(
        pack_kernel,
        out_shape=jax.ShapeDtypeStruct((siblings, SEND_ROWS, 128), BF16),
        in_specs=[whole(pltpu.HBM)] * 6,
        out_specs=whole(),
        scratch_shapes=[pltpu.SMEM((siblings,), jnp.int32)]
        + held
        + [pltpu.SemaphoreType.DMA((6,)), rows_bc],
        **params_of(60, 1_000_000, 2_000_000),
    )(*sources)
    got = lax.all_to_all(send, "sibling", split_axis=0, concat_axis=0, tiled=True)

    pages = page_table.shape[1]
    prefix = pl.pallas_call(
        prefix_kernel,
        out_shape=jax.ShapeDtypeStruct((PREFIX_ARRAYS, pages * 128, AHDIM), BF16),
        grid_spec=pltpu.PrefetchScalarGridSpec(
            num_scalar_prefetch=1,
            grid=(pages,),
            in_specs=[pl.BlockSpec((1, 256, AHDIM), lambda i, table: (table[0, i], 0, 0))],
            out_specs=pl.BlockSpec((2, 128, AHDIM), lambda i, table: (0, i, 0)),
            scratch_shapes=[pltpu.VMEM((256, AHDIM), F32)],
        ),
        **params_of(60, 4_000_000, 8_000_000),
    )(page_table, pool)

    back, old_rows = pl.pallas_call(
        parent_kernel,
        out_shape=(
            jax.ShapeDtypeStruct((siblings, CAP, tokens, channels + widths), BF16),
            jax.ShapeDtypeStruct((HISTORY_ROOM, HIST_ROWS, 128), BF16),
        ),
        in_specs=[whole()] * 3 + [whole(pltpu.HBM)] * 2,
        out_specs=(whole(pltpu.HBM), whole(pltpu.HBM)),
        scratch_shapes=[
            pltpu.VMEM((pages * 128, AHDIM), BF16),
            pltpu.VMEM((pages * 128, 2 * AHDIM), BF16),
            pltpu.VMEM((channels, state), F32),
            pltpu.VMEM((siblings, CAP, tokens, channels), BF16),
            pltpu.VMEM((siblings // 2, 2, CAP, tokens, widths), BF16),
            pltpu.VMEM((siblings // 2, 64, AHDIM), F32),
            pltpu.SemaphoreType.DMA((3,)),
            pltpu.SemaphoreType.DMA((2 + siblings // 2,)),
        ],
        **params_of(50, 6_000_000_000, 8_000_000, 4_000_000),
    )(got, conv_bc, kernel_bc, prefix, flat_state)
    returned = lax.all_to_all(back, "sibling", split_axis=0, concat_axis=0, tiled=True)

    wide = jax.ShapeDtypeStruct((children, tokens, channels), F32)
    within, fade, gate = pl.pallas_call(
        child_kernel,
        out_shape=(
            wide,
            jax.ShapeDtypeStruct((children * tokens, 128), BF16),
            jax.ShapeDtypeStruct((GATE_ROOM,) + reply_gate.shape[1:], BF16),
        ),
        in_specs=[whole(pltpu.SMEM), whole(pltpu.HBM)] + [whole()] * 6 + [whole(pltpu.HBM)],
        out_specs=(whole(), whole(), whole(pltpu.HBM)),
        scratch_shapes=[
            pltpu.VMEM((siblings, HIST_ROWS, 128), BF16),
            pltpu.VMEM((children * tokens, channels + 2 * state), F32),
            pltpu.VMEM((8 * children * tokens, 128), BF16),
            rows_bc,
            pltpu.SemaphoreType.DMA,
            pltpu.SemaphoreType.DMA,
        ],
        **params_of(44, 600_000_000, 8_000_000, 1_000_000),
    )(fork, old_rows, reply_x, bc, reply_dt, kernel_x, kernel_bc, params, reply_gate)

    mamba = jax.ShapeDtypeStruct((children, tokens, channels), BF16)
    attn = jax.ShapeDtypeStruct((children, tokens, widths), BF16)
    return pl.pallas_call(
        finish_kernel,
        out_shape=(mamba, attn),
        in_specs=[whole(pl.ANY)] * 2 + [whole()] * 4 + [whole(pltpu.HBM)],
        out_specs=(whole(pltpu.HBM), whole(pltpu.HBM)),
        scratch_shapes=[
            pltpu.SMEM((siblings,), jnp.int32),
            fork_held,
            fork_held,
            pltpu.VMEM(reply_gate.shape, BF16),
            pltpu.VMEM(wide.shape, F32),
            pltpu.VMEM(mamba.shape, BF16),
            pltpu.VMEM(attn.shape, BF16),
            pltpu.SemaphoreType.DMA((3,)),
            pltpu.SemaphoreType.DMA((2, 4)),
        ],
        **params_of(46, 10_000_000, 6_000_000),
    )(fork, lengths, returned, gain, fade, within, gate)


def solution(mesh):
    return jax.shard_map(
        local,
        mesh=mesh,
        in_specs=(
            P(("replica", "sibling"), None, "tensor"),
            P(("replica", "sibling"), None, None, "tensor"),
            P(("replica", "sibling"), None, "tensor"),
            P(("replica", "sibling"), None, "tensor"),
            P(("replica", "sibling"), None, "tensor"),
            P(("replica", "sibling"), None, None, "tensor"),
            P(("replica", "sibling")),
            P(("replica", "sibling"), None),
            P(("replica", "sibling"), "tensor", None, None),
            P(("replica", "sibling"), None, "tensor"),
            P(("replica", "sibling"), None, None, "tensor"),
            P(("replica", "sibling"), None, None, "tensor"),
            P(("replica", "sibling"), None),
            P(None, "tensor"),
            P(None, None, "tensor"),
            P("tensor"),
            P("tensor"),
            P("tensor"),
            P("tensor"),
        ),
        out_specs=(
            P(("replica", "sibling"), None, "tensor"),
            P(("replica", "sibling"), None, "tensor"),
        ),
        check_vma=False,
    )
```
